256 devices in a mesh: seq: 64 (over x, z, core), ch: 4 (over y).
Axes of the slice: x: 4, y: 4, z: 8, core: 2. Of those that a mesh axis runs over, the one named last changes fastest.
Arguments:
- query_proj: bfloat16 [8192, 2048], P('seq', 'ch'), may hold values from -6 to 6
- key_proj: bfloat16 [8192, 2048], P('seq', 'ch'), may hold values from -6 to 6
- value_proj: bfloat16 [8192, 2048], P('seq', 'ch'), may hold values from -6 to 6
- filters: bfloat16 [8192, 2048], P('seq', 'ch'), may hold values from -1.3 to 1.3
- out_weight: bfloat16 [2048, 4096], P('ch'), may hold values from -0.125 to 0.125
- grad_out: bfloat16 [8192, 4096], P('seq', 'ch'), may hold values from -6 to 6
Outputs:
- output: bfloat16 [8192, 4096], P('seq', 'ch')
- grad_query: bfloat16 [8192, 2048], P('seq', 'ch')
- grad_key: bfloat16 [8192, 2048], P('seq', 'ch')
- grad_value: bfloat16 [8192, 2048], P('seq', 'ch')
- grad_filter: float32 [8192, 2048], P('seq', 'ch')
- grad_weight: float32 [2048, 4096], P('ch', 'seq')
The draws below stay inside these ranges and needn't reach their ends.
All inputs are finite; a program needn't handle non-finite values.
Results may differ from the reference program's by a relative error of at most 0.02.
Values may be sent and summed in bfloat16 or wider, within the bound.
A program may use at most 128 MiB of HBM per device.

```python
import math
import jax
import jax.numpy as jnp
from jax import lax

C = 2048
E = 4096
TOKENS = 8192


def draw_filters(key, part):
    key = jax.random.fold_in(key, 11)
    keys_all = jax.random.split(key, 4)
    picked = jax.random.uniform(keys_all[0], (C,))
    share = 0.5
    slow_log = jax.random.uniform(keys_all[1], (C,), minval=math.log(0.1 / TOKENS), maxval=math.log(2.3 / TOKENS))
    fast_log = jax.random.uniform(keys_all[2], (C,), minval=math.log(0.02), maxval=math.log(0.05))
    rates = jnp.where(picked < share, jnp.exp(slow_log), jnp.exp(fast_log))
    spread = jnp.sqrt(2.0 * rates / (1.0 - jnp.exp(-2.0 * rates * TOKENS)))
    offsets = jnp.arange(TOKENS, dtype=jnp.float32)[:, None]
    noise = jnp.clip(jax.random.normal(keys_all[3], (TOKENS, C)), -4.0, 4.0)
    taps = noise * spread[None, :] * jnp.exp(-rates[None, :] * offsets)
    return taps.astype(jnp.float32).astype(jnp.bfloat16)


def levels(rng, shape, pieces, least, top_value):
    def one(position, shards_of):
        draws = jax.random.uniform(jax.random.fold_in(jax.random.fold_in(rng, 6), position), (shards_of,), jnp.float32, least / len(pieces), top_value / len(pieces))
        return jnp.repeat(jnp.exp(draws), shape[position] // shards_of).reshape((-1,) + (1,) * (len(shape) - position - 1))

    level = one(*pieces[0])
    for cut in pieces[1:]:
        level = level * one(*cut)
    return level


def scatter_about(rng, dims, width, limit, pieces=(), kind=jnp.bfloat16):
    drawn = jax.random.normal(rng, dims, jnp.float32) * width
    if len(pieces) > 0:
        drawn = levels(rng, dims, pieces, -0.22, 0.18) * drawn
    return jnp.clip(drawn, min=-limit, max=limit).astype(kind)


def setup_inputs(seed: int = 0) -> dict:
    key_of = jax.random.split(jax.random.key(seed), 7)
    query_proj = scatter_about(key_of[0], (TOKENS, C), 1.0, 6.0, ((0, 64), (1, 4)))
    key_proj = scatter_about(key_of[1], (TOKENS, C), 1.0, 6.0, ((0, 64), (1, 4)))
    value_proj = scatter_about(key_of[2], (TOKENS, C), 1.0, 6.0, ((0, 64), (1, 4)))
    filters = draw_filters(jax.random.fold_in(key_of[6], 71), 0)
    out_weight = scatter_about(key_of[4], (C, E), C ** -0.5, 0.125, ((0, 4),))
    grad_out = scatter_about(key_of[5], (TOKENS, E), 1.0, 6.0, ((0, 64), (1, 4)))
    return {"query_proj": query_proj, "key_proj": key_proj, "value_proj": value_proj, "filters": filters, "out_weight": out_weight, "grad_out": grad_out}


def causal_block(gated_block, filter_block, grad_block):
    length = gated_block.shape[0]
    padded = 2 * length
    gated_spec = jnp.fft.rfft(gated_block, n=padded, axis=0)
    filter_spec = jnp.fft.rfft(filter_block, n=padded, axis=0)
    grad_spec = jnp.fft.rfft(grad_block, n=padded, axis=0)
    conv = jnp.fft.irfft(gated_spec * filter_spec, n=padded, axis=0)[:length]
    grad_gated = jnp.fft.irfft(grad_spec * jnp.conj(filter_spec), n=padded, axis=0)[:length]
    grad_filter = jnp.fft.irfft(grad_spec * jnp.conj(gated_spec), n=padded, axis=0)[:length]
    return conv, grad_gated, grad_filter


def reference(query_proj, key_proj, value_proj, filters, out_weight, grad_out):
    block = math.gcd(C, 128)
    count = C // block

    def to_blocks(signal):
        return signal.astype(jnp.float32).reshape(TOKENS, count, block).transpose(1, 0, 2)

    def from_blocks(stacked):
        return stacked.transpose(1, 0, 2).reshape(TOKENS, C)

    gated = (key_proj.astype(jnp.float32) * value_proj.astype(jnp.float32)).astype(jnp.bfloat16)
    grad_mixed = jnp.dot(grad_out, out_weight.T, preferred_element_type=jnp.float32)
    grad_conv = (grad_mixed * query_proj.astype(jnp.float32)).astype(jnp.bfloat16)
    conv, grad_gated, grad_filter = lax.map(
        lambda items: causal_block(items[0], items[1], items[2]),
        (to_blocks(gated), to_blocks(filters), to_blocks(grad_conv)))
    conv = from_blocks(conv)
    grad_gated = from_blocks(grad_gated)
    scale = TOKENS ** -0.5
    grad_filter = from_blocks(grad_filter) * scale
    mixed = (query_proj.astype(jnp.float32) * conv).astype(jnp.bfloat16)
    output = jnp.dot(mixed, out_weight, preferred_element_type=jnp.float32).astype(jnp.bfloat16)
    grad_query = (grad_mixed * conv).astype(jnp.bfloat16)
    grad_weight = jnp.dot(mixed.T, grad_out, preferred_element_type=jnp.float32) * scale
    grad_key = (grad_gated * value_proj.astype(jnp.float32)).astype(jnp.bfloat16)
    grad_value = (grad_gated * key_proj.astype(jnp.float32)).astype(jnp.bfloat16)
    return output, grad_query, grad_key, grad_value, grad_filter, grad_weight
```

```python
import functools

import jax
import jax.numpy as jnp
import numpy as np
from jax import lax
from jax.experimental import pallas as pl
from jax.experimental.pallas import tpu as pltpu
from jax.sharding import PartitionSpec as P

F32 = jnp.float32
BF16 = jnp.bfloat16
MESH = pl.DeviceIdType.MESH
GRID = {64: (4, 8, 2), 8: (2, 2, 2)}


def tables(outer, inner):
    length = outer * inner
    i = np.arange(outer)
    j = np.arange(inner)
    first = 2.0 * np.pi * i[:, None] * (i[None, :] + 0.25) / outer
    twist = 2.0 * np.pi * j[None, :] * (i[:, None] + 0.25) / length
    second = 2.0 * np.pi * (j[:, None] * j[None, :] % inner) / inner
    cos, sin = np.cos(second), np.sin(second)
    outer_fwd = np.concatenate([np.cos(first).T, -np.sin(first).T], 0)
    inner_fwd = np.block([[cos, -sin], [sin, cos]])
    outer_bwd = np.concatenate([np.cos(first), -np.sin(first)], 1) / length
    found = (outer_fwd, inner_fwd, inner_fwd.T, outer_bwd, np.cos(twist), np.sin(twist))
    return [t.astype(np.float32) for t in found]


def halves(table):
    high = table.astype(BF16)
    return high, (table - high.astype(F32)).astype(BF16)


def split_wide(real, imag):
    wide = jnp.concatenate([real, imag], axis=1)
    high = wide.astype(BF16)
    low = (wide - high.astype(F32)).astype(BF16)
    return jnp.concatenate([high, low, high], axis=1)


def dot(a, b):
    return jnp.dot(a, b, preferred_element_type=F32)


def kernel(
    sizes,
    q_ref, k_ref, v_ref, f_ref, w_hbm, go_ref,
    fo_in, fi_in, bi_in, bo_in, cos_ref, sin_ref,
    out_ref, gq_ref, gk_ref, gv_ref, gf_ref, gw_ref,
    fo_ref, fi_ref, bi_ref, bo_ref, w_ref, send_a, recv_a, send_b, recv_b, send_c, recv_c, send_d, recv_d,
    wide, spec_g, spec_f, spec_h, zbuf, full, full_t, mix_send, mix_recv,
    grad_recv, part_send, part_own, part_recv, out_send, out_recv, out_own, gm_t, q_t,
    load_sem, send_sem, recv_sem,
):
    nx, nz, ns, ny, rows, scale = sizes
    me = lax.axis_index("seq")
    my = lax.axis_index("ch")
    my_x, my_z, my_k = me // (2 * nz), me // 2 % nz, me % 2
    group = nx * 2
    place = my_x * 2 + my_k
    chans = ns * 8

    def peer(step):
        return lax.rem(me + step, ns)

    def member(step):
        other = lax.rem(place + step, group)
        return other, (other // 2 * nz + my_z) * 2 + other % 2

    load = pltpu.make_async_copy(w_hbm, w_ref, load_sem)
    load.start()

    barrier = pltpu.get_barrier_semaphore()

    def greet(step, carry):
        pl.semaphore_signal(barrier, inc=1, device_id={"seq": peer(step)}, device_id_type=MESH)
        return carry

    lax.fori_loop(1, ns, greet, 0)
    for step in range(1, ny):
        pl.semaphore_signal(barrier, inc=1, device_id={"ch": lax.rem(my + step, ny)}, device_id_type=MESH)

    gated = k_ref[...].astype(F32) * v_ref[...].astype(F32)
    gated_t = gated.T.reshape(ns, 8, rows)
    taps_t = f_ref[...].astype(F32).T.reshape(ns, 8, rows)
    send_a[...] = jnp.concatenate([gated_t, taps_t], axis=1).astype(BF16)
    recv_a[me] = send_a[me]
    full[my] = go_ref[...]
    pl.semaphore_wait(barrier, ns - 1 + ny - 1)

    def exchange(send, recv, index, wide_slots):
        def slot(ref, i, count=1):
            if wide_slots:
                return ref.at[pl.ds(pl.multiple_of(i * 8, 8), 8 * count)]
            return ref.at[pl.ds(i, count)]

        def start(step, carry):
            other = peer(step)
            pltpu.make_async_remote_copy(
                src_ref=slot(send, other), dst_ref=slot(recv, me),
                send_sem=send_sem.at[index], recv_sem=recv_sem.at[index],
                device_id={"seq": other}, device_id_type=MESH,
            ).start()
            return carry

        lax.fori_loop(1, ns, start, 0)
        return pltpu.make_async_remote_copy(
            src_ref=slot(send, 0, ns - 1), dst_ref=slot(recv, 0, ns - 1),
            send_sem=send_sem.at[index], recv_sem=recv_sem.at[index],
            device_id={"seq": peer(1)}, device_id_type=MESH,
        )

    def gather_ch(send, recv, index):
        for step in range(1, ny):
            other = lax.rem(my + step, ny)
            pltpu.make_async_remote_copy(
                src_ref=send(other), dst_ref=recv.at[my],
                send_sem=send_sem.at[index], recv_sem=recv_sem.at[index],
                device_id={"ch": other}, device_id_type=MESH,
            ).start()
        return pltpu.make_async_remote_copy(
            src_ref=recv.at[pl.ds(0, ny - 1)], dst_ref=recv.at[pl.ds(0, ny - 1)],
            send_sem=send_sem.at[index], recv_sem=recv_sem.at[index],
            device_id={"ch": lax.rem(my + 1, ny)}, device_id_type=MESH,
        )

    moved_a = exchange(send_a, recv_a, 0, False)
    moved_full = gather_ch(lambda other: go_ref, full, 1)
    high, low = halves(fo_in[...])
    fo_ref[...] = jnp.concatenate([high, low], axis=1)
    high, low = halves(fi_in[...])
    fi_ref[...] = jnp.concatenate([high, high, low], axis=0)
    high, low = halves(bi_in[...])
    bi_ref[...] = jnp.concatenate([high, high, low], axis=0)
    high, low = halves(bo_in[...])
    bo_ref[...] = jnp.concatenate([high, high, low], axis=1)
    q_t[...] = q_ref[...].astype(F32).T

    def spectra(count, base, spec, spec_base, signals):
        for s in range(0, signals, 2):
            pair = [wide[pl.ds(base + s + u, ns, stride=count), :] for u in range(2)]
            block = jnp.concatenate(pair, axis=1).astype(BF16)
            stage = dot(fo_ref[...], jnp.concatenate([block, block], axis=0))
            for u in range(2):
                re = stage[:ns, u * rows:(u + 1) * rows]
                im = stage[ns:, u * rows:(u + 1) * rows]
                cos, sin = cos_ref[...], sin_ref[...]
                zbuf[pl.ds((s + u) * ns, ns), :] = split_wide(re * cos + im * sin, im * cos - re * sin)
        spec[...] = dot(zbuf[...], fi_ref[...])

    def inverse(left, right, conj, dst, count, base):
        n = rows
        for s in range(8):
            part = pl.ds(s * ns, ns)
            lr, li = left[part, :n], left[part, n:]
            rr, ri = right[part, :n], right[part, n:]
            if conj:
                zbuf[part, :] = split_wide(lr * rr + li * ri, li * rr - lr * ri)
            else:
                zbuf[part, :] = split_wide(lr * rr - li * ri, li * rr + lr * ri)
        full_stage = dot(zbuf[...], bi_ref[...])
        for s in range(0, 8, 2):
            cols = []
            for u in range(2):
                re = full_stage[(s + u) * ns:(s + u + 1) * ns, :n]
                im = full_stage[(s + u) * ns:(s + u + 1) * ns, n:]
                cos, sin = cos_ref[...], sin_ref[...]
                turned = jnp.concatenate([re * cos - im * sin, im * cos + re * sin], axis=0)
                high = turned.astype(BF16)
                low = (turned - high.astype(F32)).astype(BF16)
                cols.append(jnp.concatenate([high, low, high], axis=0))
            back = dot(bo_ref[...], jnp.concatenate(cols, axis=1))
            for u in range(2):
                dst[pl.ds(base + s + u, ns, stride=count), :] = back[:, u * n:(u + 1) * n]

    moved_a.wait_recv()
    wide[...] = recv_a[...].astype(F32).reshape(ns * 16, rows)
    spectra(16, 0, spec_g, 0, 8)
    spectra(16, 8, spec_f, 0, 8)
    inverse(spec_g, spec_f, False, send_b, 8, 0)
    recv_b[pl.ds(pl.multiple_of(me * 8, 8), 8), :] = send_b[pl.ds(pl.multiple_of(me * 8, 8), 8), :]
    moved_b = exchange(send_b, recv_b, 2, True)

    moved_full.wait_recv()
    width = full.shape[2]
    cut = width // (2 * nz)
    for j in range(ny):
        full_t[j] = full[j].T.reshape(nz, 2, cut, rows)
    for step in range(1, group):
        other, device = member(step)
        pltpu.make_async_remote_copy(
            src_ref=full_t.at[other // 2, :, other % 2], dst_ref=grad_recv.at[place],
            send_sem=send_sem.at[5], recv_sem=recv_sem.at[5],
            device_id={"seq": device}, device_id_type=MESH,
        ).start()
    grad_recv[place] = full_t[my_x, :, my_k]
    load.wait()
    gm = jnp.zeros((chans, rows), F32)
    for j in range(ny):
        gm += dot(w_ref[:, j * width:(j + 1) * width], full_t[j].reshape(width, rows))
    gm_t[...] = gm
    send_c[...] = (gm * q_t[...]).astype(BF16).astype(F32)
    recv_c[pl.ds(pl.multiple_of(me * 8, 8), 8), :] = send_c[pl.ds(pl.multiple_of(me * 8, 8), 8), :]
    moved_c = exchange(send_c, recv_c, 3, True)

    moved_b.wait_recv()
    gq_ref[...] = (gm_t[...] * recv_b[...]).T.astype(BF16)
    mixed = (q_t[...] * recv_b[...]).T.astype(BF16)
    mix_send[...] = mixed
    mix_recv[place] = mixed
    for step in range(1, group):
        other, device = member(step)
        pltpu.make_async_remote_copy(
            src_ref=mix_send, dst_ref=mix_recv.at[place],
            send_sem=send_sem.at[6], recv_sem=recv_sem.at[6],
            device_id={"seq": device}, device_id_type=MESH,
        ).start()
    for step in range(1, ny):
        other = lax.rem(my + step, ny)
        columns = pl.ds(pl.multiple_of(other * width, width), width)
        out_send[other] = dot(mix_send[...], w_ref[:, columns]).astype(BF16)
    moved_out = gather_ch(lambda other: out_send.at[other], out_recv, 7)
    out_own[...] = dot(mix_send[...], w_ref[:, pl.ds(pl.multiple_of(my * width, width), width)])

    moved_c.wait_recv()
    wide[pl.ds(0, ns * 8), :] = recv_c[...]
    spectra(8, 0, spec_h, 0, 8)
    inverse(spec_h, spec_f, True, wide, 16, 0)
    inverse(spec_h, spec_g, True, wide, 16, 8)
    send_d[...] = wide[...].reshape(ns, 16, rows).astype(BF16)
    recv_d[me] = send_d[me]
    moved_d = exchange(send_d, recv_d, 4, False)

    def group_wait(send, recv, index):
        return pltpu.make_async_remote_copy(
            src_ref=send, dst_ref=recv, send_sem=send_sem.at[index], recv_sem=recv_sem.at[index],
            device_id={"seq": member(1)[1]}, device_id_type=MESH,
        )

    moved_grad = group_wait(grad_recv.at[pl.ds(0, group - 1)], grad_recv.at[pl.ds(0, group - 1)], 5)
    moved_mix = group_wait(mix_recv.at[pl.ds(0, group - 1)], mix_recv.at[pl.ds(0, group - 1)], 6)
    moved_grad.wait_recv()
    moved_mix.wait_recv()
    columns = jnp.concatenate([grad_recv[i].reshape(nz * cut, rows) for i in range(group)], axis=1)
    part = dot(columns, mix_recv[...].reshape(group * rows, chans))
    part_send[...] = part.astype(BF16).reshape(nz, cut, chans)
    part_recv[my_z] = part_send[my_z]
    for step in range(1, nz):
        other = lax.rem(my_z + step, nz)
        pltpu.make_async_remote_copy(
            src_ref=part_send.at[other], dst_ref=part_recv.at[my_z],
            send_sem=send_sem.at[8], recv_sem=recv_sem.at[8],
            device_id={"seq": (my_x * nz + other) * 2 + my_k}, device_id_type=MESH,
        ).start()
    moved_part = pltpu.make_async_remote_copy(
        src_ref=part_recv.at[pl.ds(0, nz - 1)], dst_ref=part_recv.at[pl.ds(0, nz - 1)],
        send_sem=send_sem.at[8], recv_sem=recv_sem.at[8],
        device_id={"seq": (my_x * nz + lax.rem(my_z + 1, nz)) * 2 + my_k}, device_id_type=MESH,
    )

    moved_out.wait_recv()
    total = out_own[...]
    for step in range(1, ny):
        total += out_recv[lax.rem(my + step, ny)].astype(F32)
    out_ref[...] = total.astype(BF16)

    moved_d.wait_recv()
    back = recv_d[...].astype(F32)
    gg = back[:, :8].reshape(chans, rows).T
    gk_ref[...] = (gg * v_ref[...].astype(F32)).astype(BF16)
    gv_ref[...] = (gg * k_ref[...].astype(F32)).astype(BF16)
    gf_ref[...] = back[:, 8:].reshape(chans, rows).T * scale

    moved_part.wait_recv()
    weight = part_recv[0].astype(F32)
    for i in range(1, nz):
        weight += part_recv[i].astype(F32)
    gw_ref[...] = weight * scale

    for moved in (moved_a, moved_b, moved_c, moved_d, moved_full, moved_out, moved_grad, moved_mix, moved_part):
        moved.wait_send()


def solution(mesh):
    ns, ny = mesh.shape["seq"], mesh.shape["ch"]
    nx, nz, _ = GRID[ns]

    def shards(q, k, v, f, w, g):
        rows, chans = q.shape
        width = g.shape[1]
        cut = width // (2 * nz)
        group = nx * 2
        consts = tables(ns, rows)
        vm = pltpu.VMEM
        sizes = (nx, nz, ns, ny, rows, (ns * rows) ** -0.5)
        tok = lambda dtype: jax.ShapeDtypeStruct((rows, chans), dtype)
        *rest, gw = pl.pallas_call(
            functools.partial(kernel, sizes),
            out_shape=(
                jax.ShapeDtypeStruct((rows, width), BF16), tok(BF16), tok(BF16), tok(BF16), tok(F32),
                jax.ShapeDtypeStruct((cut, chans), F32),
            ),
            in_specs=[pl.BlockSpec(memory_space=pltpu.VMEM)] * 4
            + [pl.BlockSpec(memory_space=pl.ANY)]
            + [pl.BlockSpec(memory_space=pltpu.VMEM)] * 7,
            out_specs=(pl.BlockSpec(memory_space=pltpu.VMEM),) * 6,
            scratch_shapes=[
                vm((2 * ns, 2 * ns), BF16), vm((6 * rows, 2 * rows), BF16),
                vm((6 * rows, 2 * rows), BF16), vm((ns, 6 * ns), BF16),
                vm(w.shape, BF16),
                vm((ns, 16, rows), BF16), vm((ns, 16, rows), BF16),
                vm((chans, rows), F32), vm((chans, rows), F32),
                vm((chans, rows), F32), vm((chans, rows), F32),
                vm((ns, 16, rows), BF16), vm((ns, 16, rows), BF16),
                vm((ns * 16, rows), F32),
                vm((chans, 2 * rows), F32), vm((chans, 2 * rows), F32), vm((chans, 2 * rows), F32),
                vm((chans, 6 * rows), BF16),
                vm((ny, rows, width), BF16), vm((ny, nz, 2, cut, rows), BF16),
                vm((rows, chans), BF16), vm((group, rows, chans), BF16),
                vm((group, nz, cut, rows), BF16),
                vm((nz, cut, chans), BF16), vm((8, 128), F32), vm((nz, cut, chans), BF16),
                vm((ny, rows, width), BF16), vm((ny, rows, width), BF16), vm((rows, width), F32),
                vm((chans, rows), F32), vm((chans, rows), F32),
                pltpu.SemaphoreType.DMA, pltpu.SemaphoreType.DMA((9,)), pltpu.SemaphoreType.DMA((9,)),
            ],
            compiler_params=pltpu.CompilerParams(
                collective_id=0, has_side_effects=True, vmem_limit_bytes=48 * 1024 * 1024
            ),
        )(q, k, v, f, w, g, *consts)
        return (*rest, gw.T)

    tokens = P("seq", "ch")
    return jax.shard_map(
        shards,
        mesh=mesh,
        in_specs=(tokens, tokens, tokens, tokens, P("ch", None), tokens),
        out_specs=(tokens, tokens, tokens, tokens, tokens, P("ch", "seq")),
        check_vma=False,
    )
```

```python
import functools

import jax
import jax.numpy as jnp
import numpy as np
from jax import lax
from jax.experimental import pallas as pl
from jax.experimental.pallas import tpu as pltpu
from jax.sharding import PartitionSpec as P

F32 = jnp.float32
BF16 = jnp.bfloat16
MESH = pl.DeviceIdType.MESH
GRID = {64: (4, 8, 2), 8: (2, 2, 2)}


def tables(outer, inner, nx, nz):
    length = outer * inner
    i = np.arange(outer)
    j = np.arange(inner)
    first = 2.0 * np.pi * i[:, None] * (i[None, :] + 0.25) / outer
    twist = 2.0 * np.pi * j[None, :] * (i[:, None] + 0.25) / length
    second = 2.0 * np.pi * (j[:, None] * j[None, :] % inner) / inner
    cos, sin = np.cos(second), np.sin(second)
    packed = np.zeros((inner + 5 * outer, 2 * inner))
    packed[:inner] = np.concatenate([cos, sin], 1)
    packed[inner:inner + outer] = np.concatenate([np.cos(twist), np.sin(twist)], 1)
    packed[inner + outer:inner + 3 * outer, :outer] = np.concatenate([np.cos(first).T, -np.sin(first).T], 0)
    back = np.concatenate([np.cos(first), -np.sin(first)], 1) / length
    packed[inner + 3 * outer:inner + 4 * outer, :2 * outer] = back
    packed[inner + 4 * outer:, :2 * outer] = back[i.reshape(nx, nz, 2).transpose(1, 0, 2).reshape(-1)]
    return packed.astype(np.float32)


def halves(table):
    high = table.astype(BF16)
    return high, (table - high.astype(F32)).astype(BF16)


def split_wide(real, imag):
    wide = jnp.concatenate([real, imag], axis=1)
    high = wide.astype(BF16)
    low = (wide - high.astype(F32)).astype(BF16)
    return jnp.concatenate([high, low, high], axis=1)


def dot(a, b):
    return jnp.dot(a, b, preferred_element_type=F32)


def kernel(
    sizes,
    q_hbm, k_hbm, v_hbm, f_hbm, w_hbm, go_hbm, table_hbm,
    out_ref, gq_ref, gk_ref, gv_ref, gf_ref, gw_ref,
    q_ref, k_ref, v_ref, f_ref, go_ref, table,
    fo_ref, fi_ref, bi_ref, bo_ref, bz_ref, w_ref,
    send_a, recv_a, send_b, recv_b, send_c, recv_c, send_d, recv_d,
    wide, spec_g, spec_f, spec_h, zbuf, full, full_t, q_t, q_send, q_recv,
    conv_send, conv_recv, mix_send, mix_recv, grad_recv, part_send, part_recv,
    out_send, out_recv, out_own, gm_t,
    load_sem, send_sem, recv_sem,
):
    nx, nz, ns, ny, rows, scale = sizes
    me = lax.axis_index("seq")
    my = lax.axis_index("ch")
    my_x, my_z, my_k = me // (2 * nz), me // 2 % nz, me % 2
    group = nx * 2
    place = my_x * 2 + my_k
    half = nz // 2
    chans = ns * 8
    width = go_ref.shape[1]
    cut = width // (2 * nz)

    def peer(step):
        return lax.rem(me + step, ns)

    def run_of(device):
        x, z, k = device // (2 * nz), device // 2 % nz, device % 2
        return ((z // half * 2 + k) * nx + x) * half + z % half

    def seq_of(x, z, k):
        return (x * nz + z) * 2 + k

    def remote(src, dst, index, to):
        return pltpu.make_async_remote_copy(
            src_ref=src, dst_ref=dst, send_sem=send_sem.at[index], recv_sem=recv_sem.at[index],
            device_id=to, device_id_type=MESH,
        )

    def nearby(index, ref, count):
        part = ref.at[pl.ds(0, count)]
        return remote(part, part, index, {"seq": peer(1)})

    loads = [
        pltpu.make_async_copy(src, dst, load_sem.at[i])
        for i, (src, dst) in enumerate((
            (k_hbm, k_ref), (v_hbm, v_ref), (f_hbm, f_ref), (go_hbm, go_ref),
            (table_hbm, table), (q_hbm, q_ref), (w_hbm, w_ref),
        ))
    ]
    for load in loads:
        load.start()

    barrier = pltpu.get_barrier_semaphore()

    def greet(step, carry):
        pl.semaphore_signal(barrier, inc=1, device_id={"seq": peer(step)}, device_id_type=MESH)
        return carry

    lax.fori_loop(1, ns, greet, 0)
    for step in range(1, ny):
        pl.semaphore_signal(barrier, inc=1, device_id={"ch": lax.rem(my + step, ny)}, device_id_type=MESH)

    for load in loads[:3]:
        load.wait()
    gated = k_ref[...].astype(F32) * v_ref[...].astype(F32)
    gated_t = gated.T.reshape(ns, 8, rows)
    taps_t = f_ref[...].astype(F32).T.reshape(ns, 8, rows)
    send_a[...] = jnp.concatenate([gated_t, taps_t], axis=1).astype(BF16)
    recv_a[me] = send_a[run_of(me)]
    loads[3].wait()
    pl.semaphore_wait(barrier, ns - 1 + ny - 1)

    def exchange(send, recv, index, where, there):
        def start(step, carry):
            other = peer(step)
            remote(where(send, other), there(recv, me), index, {"seq": other}).start()
            return carry

        lax.fori_loop(1, ns, start, 0)

    def slot(ref, i):
        return ref.at[i]

    def eight(ref, i):
        return ref.at[pl.ds(pl.multiple_of(i * 8, 8), 8)]

    pieces = full.shape[0]
    zs = nz // pieces
    wide_p = width // pieces
    moved_full = []
    moved_grad = []

    def send_piece(p):
        full[p, my] = go_ref[:, p * wide_p:(p + 1) * wide_p]
        for step in (1, ny - 1, *range(2, ny - 1))[:ny - 1]:
            remote(full.at[p, my], full.at[p, my], 1 + p, {"ch": lax.rem(my + step, ny)}).start()
        moved_full.append(nearby(1 + p, full.at[p], ny - 1))

    for p in range(pieces):
        send_piece(p)
    exchange(send_a, recv_a, 0, lambda ref, d: slot(ref, run_of(d)), slot)
    moved_a = nearby(0, recv_a, ns - 1)

    def members():
        for step in range(1, group):
            other = lax.rem(place + step, group)
            yield other, {"seq": seq_of(other // 2, my_z, other % 2)}

    loads[5].wait()
    q_t[...] = q_ref[...].astype(F32).T
    q_send[...] = q_t[...].astype(BF16).reshape(q_send.shape)
    for other, to in members():
        remote(q_send.at[:, other % 2, other // 2], q_recv.at[place], 9, to).start()
    moved_q = nearby(9, q_recv, group - 1)
    q_recv[place] = q_send[:, my_k, my_x]

    def pass_on(p):
        moved_full[p].wait_recv()
        span = pl.ds(p * zs, zs)
        for step in range(ny):
            j = lax.rem(my + step, ny)
            full_t[j, span] = full[p, j].T.reshape(zs, 2, cut, rows)

            @pl.when(j == my_x)
            def _():
                grad_recv[my_k, my_x, span] = full_t[j, span]

            @pl.when(j != my_x)
            def _():
                remote(
                    full_t.at[j, span], grad_recv.at[my_k, my_x, span], 5 + p, {"seq": seq_of(j, my_z, my_k)}
                ).start()
        got = grad_recv.at[0, pl.ds(0, nx - 1), span]
        moved_grad.append(remote(got, got, 5 + p, {"seq": peer(1)}))

    loads[4].wait()
    cos, sin = table[:rows, :rows], table[:rows, rows:]
    high, low = halves(table[rows + ns:rows + 3 * ns, :ns])
    fo_ref[...] = jnp.concatenate([high, low], axis=1)
    high, low = halves(jnp.concatenate([jnp.concatenate([cos, -sin], 1), jnp.concatenate([sin, cos], 1)], 0))
    fi_ref[...] = jnp.concatenate([high, high, low], axis=0)
    high, low = halves(jnp.concatenate([jnp.concatenate([cos, sin], 1), jnp.concatenate([-sin, cos], 1)], 0))
    bi_ref[...] = jnp.concatenate([high, high, low], axis=0)
    high, low = halves(table[rows + 3 * ns:rows + 4 * ns, :2 * ns])
    bo_ref[...] = jnp.concatenate([high, high, low], axis=1)
    high, low = halves(table[rows + 4 * ns:, :2 * ns])
    bz_ref[...] = jnp.concatenate([high, high, low], axis=1)
    turn = pl.ds(rows, ns)

    def spectra(count, base, spec):
        for s in range(0, 8, 2):
            pair = [wide[pl.ds(base + s + u, ns, stride=count), :] for u in range(2)]
            block = jnp.concatenate(pair, axis=1).astype(BF16)
            stage = dot(fo_ref[...], jnp.concatenate([block, block], axis=0))
            for u in range(2):
                re = stage[:ns, u * rows:(u + 1) * rows]
                im = stage[ns:, u * rows:(u + 1) * rows]
                cos, sin = table[turn, :rows], table[turn, rows:]
                zbuf[pl.ds((s + u) * ns, ns), :] = split_wide(re * cos + im * sin, im * cos - re * sin)
        spec[...] = dot(zbuf[...], fi_ref[...])

    def inverse(left, right, conj, last, dst, count, base):
        n = rows
        for s in range(8):
            part = pl.ds(s * ns, ns)
            lr, li = left[part, :n], left[part, n:]
            rr, ri = right[part, :n], right[part, n:]
            if conj:
                zbuf[part, :] = split_wide(lr * rr + li * ri, li * rr - lr * ri)
            else:
                zbuf[part, :] = split_wide(lr * rr - li * ri, li * rr + lr * ri)
        full_stage = dot(zbuf[...], bi_ref[...])
        for s in range(0, 8, 2):
            cols = []
            for u in range(2):
                re = full_stage[(s + u) * ns:(s + u + 1) * ns, :n]
                im = full_stage[(s + u) * ns:(s + u + 1) * ns, n:]
                cos, sin = table[turn, :rows], table[turn, rows:]
                turned = jnp.concatenate([re * cos - im * sin, im * cos + re * sin], axis=0)
                high = turned.astype(BF16)
                low = (turned - high.astype(F32)).astype(BF16)
                cols.append(jnp.concatenate([high, low, high], axis=0))
            back = dot(last[...], jnp.concatenate(cols, axis=1))
            for u in range(2):
                dst[pl.ds(base + s + u, ns, stride=count), :] = back[:, u * n:(u + 1) * n]

    pass_on(0)
    moved_a.wait_recv()
    wide[...] = recv_a[...].astype(F32).reshape(ns * 16, rows)
    spectra(16, 0, spec_g)
    spectra(16, 8, spec_f)
    inverse(spec_g, spec_f, False, bz_ref, send_c, 8, 0)
    send_b[...] = send_c[...].astype(BF16).reshape(nz, group * 8, rows)
    for step in range(1, nz):
        other = lax.rem(my_z + step, nz)
        remote(send_b.at[other], recv_b.at[my_z], 10, {"seq": seq_of(my_x, other, my_k)}).start()
    moved_b = nearby(10, recv_b, nz - 1)
    recv_b[my_z] = send_b[my_z]

    for p in range(1, pieces - 1):
        pass_on(p)

    moved_q.wait_recv()
    moved_b.wait_recv()
    conv = recv_b[...].astype(F32).reshape(nz, group, 8, rows)
    conv = jnp.swapaxes(conv, 0, 1).reshape(group, 2, half * 8, rows)
    mixed = (q_recv[...].astype(F32) * conv).astype(BF16)
    for p in range(2):
        mix_send[p] = mixed[:, p]
        for step in range(1, nx):
            other = lax.rem(my_x + step, nx)
            remote(mix_send.at[p], mix_recv.at[p, my_x], 11 + p, {"seq": seq_of(other, my_z, my_k)}).start()
    conv_send[...] = conv.astype(BF16)
    for other, to in members():
        remote(conv_send.at[other], conv_recv.at[:, my_k, my_x], 13, to).start()
    moved_mix = [nearby(11 + p, mix_recv.at[p], nx - 1) for p in range(2)]
    moved_conv = nearby(13, conv_send, group - 1)
    conv_recv[:, my_k, my_x] = conv_send[place]
    for p in range(2):
        mix_recv[p, my_x] = mix_send[p]

    pass_on(pieces - 1)
    loads[6].wait()
    gm = jnp.zeros((chans, rows), F32)
    for j in range(ny):
        gm += dot(w_ref[:, j * width:(j + 1) * width], full_t[j].reshape(width, rows))
    gm_t[...] = gm
    send_c[...] = (gm * q_t[...]).astype(BF16).astype(F32)
    eight(recv_c, me)[...] = eight(send_c, run_of(me))[...]
    exchange(send_c, recv_c, 14, lambda ref, d: eight(ref, run_of(d)), eight)
    moved_c = nearby(14, recv_c, 8 * (ns - 1))

    moved_conv.wait_recv()
    conv = conv_recv[...].astype(F32).reshape(chans, rows)
    gq_ref[...] = (gm_t[...] * conv).T.astype(BF16)
    mixed = (q_t[...] * conv).T.astype(BF16)
    for step in range(1, ny):
        other = lax.rem(my + step, ny)
        columns = pl.ds(pl.multiple_of(other * width, width), width)
        out_send[other] = dot(mixed, w_ref[:, columns]).astype(BF16)
        remote(out_send.at[other], out_recv.at[my], 15, {"ch": other}).start()
    moved_out = nearby(15, out_recv, ny - 1)
    out_own[...] = dot(mixed, w_ref[:, pl.ds(pl.multiple_of(my * width, width), width)])

    moved_swap = []
    for h in range(2):
        for p in range(h * pieces // 2, (h + 1) * pieces // 2):
            moved_grad[p].wait_recv()
        mine = grad_recv.at[my_k, :, pl.ds(h * half, half)]
        moved_swap.append(remote(mine, mine, 16 + h, {"seq": seq_of(my_x, my_z, 1 - my_k)}))
        moved_swap[h].start()

    moved_part = []
    for p in range(2):
        moved_mix[p].wait_recv()
        if p == 0:
            moved_swap[0].wait_recv()
            moved_swap[1].wait_recv()
        right = jnp.concatenate(
            [mix_recv[p, :, i].reshape(half * 8 * nx, rows) for i in range(group)], axis=1
        )
        for z in range(nz):
            left = jnp.concatenate(
                [grad_recv[i % 2, i // 2, z].reshape(2 * cut, rows) for i in range(group)], axis=1
            )
            part = lax.dot_general(left, right, (((1,), (1,)), ((), ())), preferred_element_type=F32)
            part_send[p, z] = part.astype(BF16).reshape(2, cut, half * 8 * nx)
        for step in range(1, 2 * nz):
            other = lax.rem(my_z * 2 + my_k + step, 2 * nz)
            remote(
                part_send.at[p, other // 2, other % 2], part_recv.at[p, my_z * 2 + my_k], 18 + p,
                {"seq": my_x * 2 * nz + other},
            ).start()
        moved_part.append(nearby(18 + p, part_recv.at[p], 2 * nz - 1))
        part_recv[p, my_z * 2 + my_k] = part_send[p, my_z, my_k]

    moved_c.wait_recv()
    wide[pl.ds(0, ns * 8), :] = recv_c[...]
    spectra(8, 0, spec_h)
    inverse(spec_h, spec_f, True, bo_ref, wide, 16, 0)
    inverse(spec_h, spec_g, True, bo_ref, wide, 16, 8)
    send_d[...] = wide[...].reshape(ns, 16, rows).astype(BF16)
    recv_d[run_of(me)] = send_d[me]
    exchange(send_d, recv_d, 20, slot, lambda ref, d: slot(ref, run_of(d)))
    moved_d = nearby(20, recv_d, ns - 1)

    moved_out.wait_recv()
    total = out_own[...]
    for step in range(1, ny):
        total += out_recv[lax.rem(my + step, ny)].astype(F32)
    out_ref[...] = total.astype(BF16)

    moved_d.wait_recv()
    back = recv_d[...].astype(F32)
    gg = back[:, :8].reshape(chans, rows).T
    gk_ref[...] = (gg * v_ref[...].astype(F32)).astype(BF16)
    gv_ref[...] = (gg * k_ref[...].astype(F32)).astype(BF16)
    gf_ref[...] = back[:, 8:].reshape(chans, rows).T * scale

    for p in range(2):
        moved_part[p].wait_recv()
        for k in range(2):
            weight = part_recv[p, k].astype(F32)
            for i in range(1, nz):
                weight += part_recv[p, 2 * i + k].astype(F32)
            lanes = half * 8 * nx
            gw_ref[:, (2 * p + k) * lanes:(2 * p + k + 1) * lanes] = weight * scale

    for moved in (
        moved_a, moved_b, moved_c, moved_d, moved_q, moved_conv, moved_out,
        *moved_full, *moved_grad, *moved_swap, *moved_mix, *moved_part,
    ):
        moved.wait_send()


def store(*refs):
    count = len(refs) // 2
    copies = [pltpu.make_async_copy(refs[i], refs[count + i], refs[-1].at[i]) for i in range(count)]
    for copy in copies:
        copy.start()
    for copy in copies:
        copy.wait()


def solution(mesh):
    ns, ny = mesh.shape["seq"], mesh.shape["ch"]
    nx, nz, _ = GRID[ns]

    def shards(q, k, v, f, w, g):
        rows, chans = q.shape
        width = g.shape[1]
        cut = width // (2 * nz)
        group = nx * 2
        run = nz * 4
        pieces = min(4, nz)
        table = tables(ns, rows, nx, nz)
        vm = pltpu.VMEM
        sizes = (nx, nz, ns, ny, rows, (ns * rows) ** -0.5)
        tok = lambda dtype: jax.ShapeDtypeStruct((rows, chans), dtype)
        results = pl.pallas_call(
            functools.partial(kernel, sizes),
            out_shape=(
                jax.ShapeDtypeStruct((rows, width), BF16), tok(BF16), tok(BF16), tok(BF16), tok(F32),
                jax.ShapeDtypeStruct((cut, chans), F32),
            ),
            in_specs=[pl.BlockSpec(memory_space=pl.ANY)] * 7,
            out_specs=(pl.BlockSpec(memory_space=pltpu.VMEM),) * 6,
            scratch_shapes=[
                vm(q.shape, BF16), vm(q.shape, BF16), vm(q.shape, BF16), vm(q.shape, BF16),
                vm(g.shape, BF16), vm(table.shape, F32),
                vm((2 * ns, 2 * ns), BF16), vm((6 * rows, 2 * rows), BF16), vm((6 * rows, 2 * rows), BF16),
                vm((ns, 6 * ns), BF16), vm((ns, 6 * ns), BF16), vm(w.shape, BF16),
                vm((ns, 16, rows), BF16), vm((ns, 16, rows), BF16),
                vm((nz, group * 8, rows), BF16), vm((nz, group * 8, rows), BF16),
                vm((chans, rows), F32), vm((chans, rows), F32),
                vm((ns, 16, rows), BF16), vm((ns, 16, rows), BF16),
                vm((ns * 16, rows), F32),
                vm((chans, 2 * rows), F32), vm((chans, 2 * rows), F32), vm((chans, 2 * rows), F32),
                vm((chans, 6 * rows), BF16),
                vm((pieces, ny, rows, width // pieces), BF16), vm((ny, nz, 2, cut, rows), BF16),
                vm((chans, rows), F32),
                vm((2, 2, nx, run, rows), BF16), vm((group, 2, run, rows), BF16),
                vm((group, 2, run, rows), BF16), vm((2, 2, nx, run, rows), BF16),
                vm((2, group, run, rows), BF16), vm((2, nx, group, run, rows), BF16),
                vm((2, nx, nz, 2, cut, rows), BF16),
                vm((2, nz, 2, cut, run * nx), BF16), vm((2, 2 * nz, cut, run * nx), BF16),
                vm((ny, rows, width), BF16), vm((ny, rows, width), BF16), vm((rows, width), F32),
                vm((chans, rows), F32),
                pltpu.SemaphoreType.DMA((7,)), pltpu.SemaphoreType.DMA((21,)), pltpu.SemaphoreType.DMA((21,)),
            ],
            compiler_params=pltpu.CompilerParams(
                collective_id=0, has_side_effects=True, vmem_limit_bytes=56 * 1024 * 1024
            ),
        )(q, k, v, f, w, g, table)
        *rest, gw = pl.pallas_call(
            store,
            out_shape=tuple(jax.ShapeDtypeStruct(r.shape, r.dtype) for r in results),
            in_specs=[pl.BlockSpec(memory_space=pltpu.VMEM)] * 6,
            out_specs=(pl.BlockSpec(memory_space=pl.ANY),) * 6,
            scratch_shapes=[pltpu.SemaphoreType.DMA((6,))],
        )(*results)
        return (*rest, gw.T)

    tokens = P("seq", "ch")
    return jax.shard_map(
        shards,
        mesh=mesh,
        in_specs=(tokens, tokens, tokens, tokens, P("ch", None), tokens),
        out_specs=(tokens, tokens, tokens, tokens, tokens, P("ch", "seq")),
        check_vma=False,
    )
```

```python
import functools

import jax
import jax.numpy as jnp
import numpy as np
from jax import lax
from jax.experimental import pallas as pl
from jax.experimental.pallas import tpu as pltpu
from jax.sharding import PartitionSpec as P

F32 = jnp.float32
BF16 = jnp.bfloat16
MESH = pl.DeviceIdType.MESH
GRID = {64: (4, 8, 2), 16: (2, 4, 2)}


def tables(outer, inner, nx, nz):
    length = outer * inner
    i = np.arange(outer)
    j = np.arange(inner)
    first = 2.0 * np.pi * i[:, None] * (i[None, :] + 0.25) / outer
    twist = 2.0 * np.pi * j[None, :] * (i[:, None] + 0.25) / length
    second = 2.0 * np.pi * (j[:, None] * j[None, :] % inner) / inner
    cos, sin = np.cos(second), np.sin(second)
    packed = np.zeros((inner + 5 * outer, 2 * inner))
    packed[:inner] = np.concatenate([cos, sin], 1)
    packed[inner:inner + outer] = np.concatenate([np.cos(twist), np.sin(twist)], 1)
    packed[inner + outer:inner + 3 * outer, :outer] = np.concatenate([np.cos(first).T, -np.sin(first).T], 0)
    back = np.concatenate([np.cos(first), -np.sin(first)], 1) / length
    packed[inner + 3 * outer:inner + 4 * outer, :2 * outer] = back
    packed[inner + 4 * outer:, :2 * outer] = back[i.reshape(nx, nz, 2).transpose(1, 0, 2).reshape(-1)]
    return packed.astype(np.float32)


def halves(table):
    high = table.astype(BF16)
    return high, (table - high.astype(F32)).astype(BF16)


def split_wide(real, imag):
    wide = jnp.concatenate([real, imag], axis=1)
    high = wide.astype(BF16)
    low = (wide - high.astype(F32)).astype(BF16)
    return jnp.concatenate([high, low, high], axis=1)


def dot(a, b):
    return jnp.dot(a, b, preferred_element_type=F32)


def kernel(
    sizes,
    q_hbm, k_hbm, v_hbm, f_hbm, w_hbm, go_hbm, table_hbm,
    out_ref, gq_ref, gk_ref, gv_ref, gf_ref, gw_ref,
    q_ref, k_ref, v_ref, f_ref, go_ref, table,
    fo_ref, fi_ref, bi_ref, bo_ref, bz_ref, w_ref,
    send_a, recv_a, send_b, recv_b, send_c, recv_c, send_d, recv_d,
    wide, spec_g, spec_f, spec_h, zbuf, full, full_t, q_t, q_send, q_recv,
    conv_send, conv_recv, mix_send, mix_recv, grad_recv, part_send, part_recv,
    out_send, out_recv, out_own, gm_t,
    load_sem, send_sem, recv_sem,
):
    nx, nz, ns, ny, rows, scale = sizes
    me = lax.axis_index("seq")
    my = lax.axis_index("ch")
    my_x, my_z, my_k = me // (2 * nz), me // 2 % nz, me % 2
    group = nx * 2
    place = my_x * 2 + my_k
    half = nz // 2
    chans = ns * 8
    width = go_ref.shape[1]
    cut = width // (2 * nz)

    def peer(step):
        return lax.rem(me + step, ns)

    def run_of(device):
        x, z, k = device // (2 * nz), device // 2 % nz, device % 2
        return ((z // half * 2 + k) * nx + x) * half + z % half

    def seq_of(x, z, k):
        return (x * nz + z) * 2 + k

    def remote(src, dst, index, to):
        return pltpu.make_async_remote_copy(
            src_ref=src, dst_ref=dst, send_sem=send_sem.at[index], recv_sem=recv_sem.at[index],
            device_id=to, device_id_type=MESH,
        )

    def nearby(index, ref, count):
        part = ref.at[pl.ds(0, count)]
        return remote(part, part, index, {"seq": peer(1)})

    loads = [
        pltpu.make_async_copy(src, dst, load_sem.at[i])
        for i, (src, dst) in enumerate((
            (k_hbm, k_ref), (v_hbm, v_ref), (f_hbm, f_ref), (go_hbm, go_ref),
            (table_hbm, table), (q_hbm, q_ref), (w_hbm, w_ref),
        ))
    ]
    for load in loads:
        load.start()

    barrier = pltpu.get_barrier_semaphore()

    def greet(step, carry):
        pl.semaphore_signal(barrier, inc=1, device_id={"seq": peer(step)}, device_id_type=MESH)
        return carry

    lax.fori_loop(1, ns, greet, 0)
    for step in range(1, ny):
        pl.semaphore_signal(barrier, inc=1, device_id={"ch": lax.rem(my + step, ny)}, device_id_type=MESH)

    for load in loads[:3]:
        load.wait()
    gated = k_ref[...].astype(F32) * v_ref[...].astype(F32)
    gated_t = gated.T.reshape(ns, 8, rows)
    taps_t = f_ref[...].astype(F32).T.reshape(ns, 8, rows)
    send_a[...] = jnp.concatenate([gated_t, taps_t], axis=1).astype(BF16)
    recv_a[me] = send_a[run_of(me)]
    loads[3].wait()
    pl.semaphore_wait(barrier, ns - 1 + ny - 1)

    def exchange(send, recv, index, where, there):
        def start(step, carry):
            other = peer(step)
            remote(where(send, other), there(recv, me), index, {"seq": other}).start()
            return carry

        lax.fori_loop(1, ns, start, 0)

    def slot(ref, i):
        return ref.at[i]

    def eight(ref, i):
        return ref.at[pl.ds(pl.multiple_of(i * 8, 8), 8)]

    pieces = half
    lows = [*range(0, half, 2), *range(1, half, 2)]
    moved_full = []
    moved_grad = []

    def send_piece(p):
        for u in range(2):
            first = (u * half + lows[p]) * 2 * cut
            full[p, my, :, u * 2 * cut:(u + 1) * 2 * cut] = go_ref[:, first:first + 2 * cut]
        for step in (1, ny - 1, *range(2, ny - 1))[:ny - 1]:
            remote(full.at[p, my], full.at[p, my], 1 + p, {"ch": lax.rem(my + step, ny)}).start()
        moved_full.append(nearby(1 + p, full.at[p], ny - 1))

    for p in range(pieces):
        send_piece(p)
    exchange(send_a, recv_a, 0, lambda ref, d: slot(ref, run_of(d)), slot)
    moved_a = nearby(0, recv_a, ns - 1)

    def members():
        for step in range(1, group):
            other = lax.rem(place + step, group)
            yield other, {"seq": seq_of(other // 2, my_z, other % 2)}

    loads[5].wait()
    q_t[...] = q_ref[...].astype(F32).T
    q_send[...] = q_t[...].astype(BF16).reshape(q_send.shape)
    for other, to in members():
        remote(q_send.at[:, other % 2, other // 2], q_recv.at[place], 9, to).start()
    moved_q = nearby(9, q_recv, group - 1)
    q_recv[place] = q_send[:, my_k, my_x]

    def pass_on(p):
        moved_full[p].wait_recv()
        low = lows[p]
        for step in range(ny):
            j = lax.rem(my + step, ny)
            full_t[j, :, low] = full[p, j].T.reshape(2, 2, cut, rows)

            @pl.when(j == my_x)
            def _():
                grad_recv[my_k, my_x, :, low] = full_t[j, :, low]

            @pl.when(j != my_x)
            def _():
                remote(
                    full_t.at[j, :, low], grad_recv.at[my_k, my_x, :, low], 5 + p, {"seq": seq_of(j, my_z, my_k)}
                ).start()
        got = grad_recv.at[0, pl.ds(0, nx - 1), :, low]
        moved_grad.append(remote(got, got, 5 + p, {"seq": peer(1)}))

    loads[4].wait()
    cos, sin = table[:rows, :rows], table[:rows, rows:]
    high, low = halves(table[rows + ns:rows + 3 * ns, :ns])
    fo_ref[...] = jnp.concatenate([high, low], axis=1)
    high, low = halves(jnp.concatenate([jnp.concatenate([cos, -sin], 1), jnp.concatenate([sin, cos], 1)], 0))
    fi_ref[...] = jnp.concatenate([high, high, low], axis=0)
    high, low = halves(jnp.concatenate([jnp.concatenate([cos, sin], 1), jnp.concatenate([-sin, cos], 1)], 0))
    bi_ref[...] = jnp.concatenate([high, high, low], axis=0)
    high, low = halves(table[rows + 3 * ns:rows + 4 * ns, :2 * ns])
    bo_ref[...] = jnp.concatenate([high, high, low], axis=1)
    high, low = halves(table[rows + 4 * ns:, :2 * ns])
    bz_ref[...] = jnp.concatenate([high, high, low], axis=1)
    turn = pl.ds(rows, ns)

    def spectra(count, base, spec):
        for s in range(0, 8, 2):
            pair = [wide[pl.ds(base + s + u, ns, stride=count), :] for u in range(2)]
            block = jnp.concatenate(pair, axis=1).astype(BF16)
            stage = dot(fo_ref[...], jnp.concatenate([block, block], axis=0))
            for u in range(2):
                re = stage[:ns, u * rows:(u + 1) * rows]
                im = stage[ns:, u * rows:(u + 1) * rows]
                cos, sin = table[turn, :rows], table[turn, rows:]
                zbuf[pl.ds((s + u) * ns, ns), :] = split_wide(re * cos + im * sin, im * cos - re * sin)
        spec[...] = dot(zbuf[...], fi_ref[...])

    def inverse(left, right, conj, last, dst, count, base):
        n = rows
        for s in range(8):
            part = pl.ds(s * ns, ns)
            lr, li = left[part, :n], left[part, n:]
            rr, ri = right[part, :n], right[part, n:]
            if conj:
                zbuf[part, :] = split_wide(lr * rr + li * ri, li * rr - lr * ri)
            else:
                zbuf[part, :] = split_wide(lr * rr - li * ri, li * rr + lr * ri)
        full_stage = dot(zbuf[...], bi_ref[...])
        for s in range(0, 8, 2):
            cols = []
            for u in range(2):
                re = full_stage[(s + u) * ns:(s + u + 1) * ns, :n]
                im = full_stage[(s + u) * ns:(s + u + 1) * ns, n:]
                cos, sin = table[turn, :rows], table[turn, rows:]
                turned = jnp.concatenate([re * cos - im * sin, im * cos + re * sin], axis=0)
                high = turned.astype(BF16)
                low = (turned - high.astype(F32)).astype(BF16)
                cols.append(jnp.concatenate([high, low, high], axis=0))
            back = dot(last[...], jnp.concatenate(cols, axis=1))
            for u in range(2):
                dst[pl.ds(base + s + u, ns, stride=count), :] = back[:, u * n:(u + 1) * n]

    pass_on(0)
    moved_a.wait_recv()
    wide[...] = recv_a[...].astype(F32).reshape(ns * 16, rows)
    spectra(16, 0, spec_g)
    spectra(16, 8, spec_f)
    inverse(spec_g, spec_f, False, bz_ref, send_c, 8, 0)
    send_b[...] = send_c[...].astype(BF16).reshape(nz, group * 8, rows)
    for step in range(1, nz):
        other = lax.rem(my_z + step, nz)
        remote(send_b.at[other], recv_b.at[my_z], 10, {"seq": seq_of(my_x, other, my_k)}).start()
    moved_b = nearby(10, recv_b, nz - 1)
    recv_b[my_z] = send_b[my_z]

    for p in range(1, pieces - 1):
        pass_on(p)

    moved_q.wait_recv()
    moved_b.wait_recv()
    conv = recv_b[...].astype(F32).reshape(nz, group, 8, rows)
    conv = jnp.swapaxes(conv, 0, 1).reshape(group, 2, half * 8, rows)
    mixed = (q_recv[...].astype(F32) * conv).astype(BF16)
    mix_send[...] = jnp.swapaxes(mixed, 0, 1)
    conv_send[...] = conv.astype(BF16)
    for other, to in members():
        remote(conv_send.at[other], conv_recv.at[:, my_k, my_x], 13, to).start()
    moved_conv = nearby(13, conv_send, group - 1)
    conv_recv[:, my_k, my_x] = conv_send[place]

    pass_on(pieces - 1)

    def swap(h):
        for p in range(h * half // 2, (h + 1) * half // 2):
            moved_grad[p].wait_recv()
            mine = grad_recv.at[my_k, :, :, lows[p]]
            remote(mine, mine, 16 + h, {"seq": seq_of(my_x, my_z, 1 - my_k)}).start()
        both = grad_recv.at[0, :, :, pl.ds(0, half // 2)]
        return remote(both, both, 16 + h, {"seq": peer(1)})

    moved_swap = [swap(0)]

    loads[6].wait()
    gm = jnp.zeros((chans, rows), F32)
    for j in range(ny):
        gm += dot(w_ref[:, j * width:(j + 1) * width], full_t[j].reshape(width, rows))
    gm_t[...] = gm
    send_c[...] = (gm * q_t[...]).astype(BF16).astype(F32)
    eight(recv_c, me)[...] = eight(send_c, run_of(me))[...]
    exchange(send_c, recv_c, 14, lambda ref, d: eight(ref, run_of(d)), eight)
    moved_c = nearby(14, recv_c, 8 * (ns - 1))

    for step in range(1, nx):
        other = lax.rem(my_x + step, nx)
        remote(mix_send, mix_recv.at[my_x], 11, {"seq": seq_of(other, my_z, my_k)}).start()
    moved_mix = nearby(11, mix_recv, nx - 1)
    mix_recv[my_x] = mix_send[...]
    moved_swap.append(swap(1))

    moved_conv.wait_recv()
    conv = conv_recv[...].astype(F32).reshape(chans, rows)
    gq_ref[...] = (gm_t[...] * conv).T.astype(BF16)
    mixed = (q_t[...] * conv).T.astype(BF16)
    for step in range(1, ny):
        other = lax.rem(my + step, ny)
        columns = pl.ds(pl.multiple_of(other * width, width), width)
        out_send[other] = dot(mixed, w_ref[:, columns]).astype(BF16)
        remote(out_send.at[other], out_recv.at[my], 15, {"ch": other}).start()
    moved_out = nearby(15, out_recv, ny - 1)
    out_own[...] = dot(mixed, w_ref[:, pl.ds(pl.multiple_of(my * width, width), width)])

    moved_c.wait_recv()
    wide[pl.ds(0, ns * 8), :] = recv_c[...]
    spectra(8, 0, spec_h)
    inverse(spec_h, spec_f, True, bo_ref, wide, 16, 0)
    inverse(spec_h, spec_g, True, bo_ref, wide, 16, 8)
    send_d[...] = wide[...].reshape(ns, 16, rows).astype(BF16)
    recv_d[run_of(me)] = send_d[me]
    exchange(send_d, recv_d, 20, slot, lambda ref, d: slot(ref, run_of(d)))
    moved_d = nearby(20, recv_d, ns - 1)

    moved_mix.wait_recv()
    right = jnp.concatenate(
        [mix_recv[:, p, i].reshape(half * 8 * nx, rows) for p in range(2) for i in range(group)], axis=1
    )
    right = jnp.concatenate([right[:, :group * rows], right[:, group * rows:]], axis=0)
    here = my_z * 2 + my_k
    for h in range(2):
        moved_swap[h].wait_recv()
        for t in range(half):
            z = lax.rem(2 * (my_z // 2 + t), nz) + h
            left = jnp.concatenate(
                [grad_recv[i % 2, i // 2, z // half, z % half].reshape(2 * cut, rows) for i in range(group)], axis=1
            )
            part = lax.dot_general(left, right, (((1,), (1,)), ((), ())), preferred_element_type=F32)
            part_send[z] = part.astype(BF16).reshape(2, cut, half * 16 * nx)
            for k in range(2):
                there = z * 2 + k

                @pl.when(there == here)
                def _():
                    part_recv[here] = part_send[z, k]

                @pl.when(there != here)
                def _():
                    remote(
                        part_send.at[z, k], part_recv.at[here], 18, {"seq": my_x * 2 * nz + there}
                    ).start()
    moved_part = nearby(18, part_recv, 2 * nz - 1)

    moved_out.wait_recv()
    total = out_own[...]
    for step in range(1, ny):
        total += out_recv[lax.rem(my + step, ny)].astype(F32)
    out_ref[...] = total.astype(BF16)

    moved_d.wait_recv()
    back = recv_d[...].astype(F32)
    gg = back[:, :8].reshape(chans, rows).T
    gk_ref[...] = (gg * v_ref[...].astype(F32)).astype(BF16)
    gv_ref[...] = (gg * k_ref[...].astype(F32)).astype(BF16)
    gf_ref[...] = back[:, 8:].reshape(chans, rows).T * scale

    moved_part.wait_recv()
    lanes = half * 8 * nx
    for k in range(2):
        weight = part_recv[k].astype(F32)
        for i in range(1, nz):
            weight += part_recv[2 * i + k].astype(F32)
        for p in range(2):
            gw_ref[:, (2 * p + k) * lanes:(2 * p + k + 1) * lanes] = weight[:, p * lanes:(p + 1) * lanes] * scale

    for moved in (
        moved_a, moved_b, moved_c, moved_d, moved_q, moved_conv, moved_out,
        *moved_full, moved_mix, moved_part, *moved_grad, *moved_swap,
    ):
        moved.wait_send()


def store(*refs):
    count = len(refs) // 2
    copies = [pltpu.make_async_copy(refs[i], refs[count + i], refs[-1].at[i]) for i in range(count)]
    for copy in copies:
        copy.start()
    for copy in copies:
        copy.wait()


def solution(mesh):
    ns, ny = mesh.shape["seq"], mesh.shape["ch"]
    nx, nz, _ = GRID[ns]

    def shards(q, k, v, f, w, g):
        rows, chans = q.shape
        width = g.shape[1]
        cut = width // (2 * nz)
        group = nx * 2
        run = nz * 4
        pieces = nz // 2
        table = tables(ns, rows, nx, nz)
        vm = pltpu.VMEM
        sizes = (nx, nz, ns, ny, rows, (ns * rows) ** -0.5)
        tok = lambda dtype: jax.ShapeDtypeStruct((rows, chans), dtype)
        results = pl.pallas_call(
            functools.partial(kernel, sizes),
            out_shape=(
                jax.ShapeDtypeStruct((rows, width), BF16), tok(BF16), tok(BF16), tok(BF16), tok(F32),
                jax.ShapeDtypeStruct((cut, chans), F32),
            ),
            in_specs=[pl.BlockSpec(memory_space=pl.ANY)] * 7,
            out_specs=(pl.BlockSpec(memory_space=pltpu.VMEM),) * 6,
            scratch_shapes=[
                vm(q.shape, BF16), vm(q.shape, BF16), vm(q.shape, BF16), vm(q.shape, BF16),
                vm(g.shape, BF16), vm(table.shape, F32),
                vm((2 * ns, 2 * ns), BF16), vm((6 * rows, 2 * rows), BF16), vm((6 * rows, 2 * rows), BF16),
                vm((ns, 6 * ns), BF16), vm((ns, 6 * ns), BF16), vm(w.shape, BF16),
                vm((ns, 16, rows), BF16), vm((ns, 16, rows), BF16),
                vm((nz, group * 8, rows), BF16), vm((nz, group * 8, rows), BF16),
                vm((chans, rows), F32), vm((chans, rows), F32),
                vm((ns, 16, rows), BF16), vm((ns, 16, rows), BF16),
                vm((ns * 16, rows), F32),
                vm((chans, 2 * rows), F32), vm((chans, 2 * rows), F32), vm((chans, 2 * rows), F32),
                vm((chans, 6 * rows), BF16),
                vm((pieces, ny, rows, width // pieces), BF16), vm((ny, 2, nz // 2, 2, cut, rows), BF16),
                vm((chans, rows), F32),
                vm((2, 2, nx, run, rows), BF16), vm((group, 2, run, rows), BF16),
                vm((group, 2, run, rows), BF16), vm((2, 2, nx, run, rows), BF16),
                vm((2, group, run, rows), BF16), vm((nx, 2, group, run, rows), BF16),
                vm((2, nx, 2, nz // 2, 2, cut, rows), BF16),
                vm((nz, 2, cut, 2 * run * nx), BF16), vm((2 * nz, cut, 2 * run * nx), BF16),
                vm((ny, rows, width), BF16), vm((ny, rows, width), BF16), vm((rows, width), F32),
                vm((chans, rows), F32),
                pltpu.SemaphoreType.DMA((7,)), pltpu.SemaphoreType.DMA((21,)), pltpu.SemaphoreType.DMA((21,)),
            ],
            compiler_params=pltpu.CompilerParams(
                collective_id=0, has_side_effects=True, vmem_limit_bytes=56 * 1024 * 1024
            ),
        )(q, k, v, f, w, g, table)
        *rest, gw = pl.pallas_call(
            store,
            out_shape=tuple(jax.ShapeDtypeStruct(r.shape, r.dtype) for r in results),
            in_specs=[pl.BlockSpec(memory_space=pltpu.VMEM)] * 6,
            out_specs=(pl.BlockSpec(memory_space=pl.ANY),) * 6,
            scratch_shapes=[pltpu.SemaphoreType.DMA((6,))],
        )(*results)
        return (*rest, gw.T)

    tokens = P("seq", "ch")
    return jax.shard_map(
        shards,
        mesh=mesh,
        in_specs=(tokens, tokens, tokens, tokens, P("ch", None), tokens),
        out_specs=(tokens, tokens, tokens, tokens, tokens, P("ch", "seq")),
        check_vma=False,
    )
```

```python
import functools

import jax
import jax.numpy as jnp
import numpy as np
from jax import lax
from jax.experimental import pallas as pl
from jax.experimental.pallas import tpu as pltpu
from jax.sharding import PartitionSpec as P

F32 = jnp.float32
BF16 = jnp.bfloat16
MESH = pl.DeviceIdType.MESH
GRID = {64: (4, 8, 2), 16: (2, 4, 2)}


def tables(outer, inner, nx, nz):
    length = outer * inner
    i = np.arange(outer)
    j = np.arange(inner)
    first = 2.0 * np.pi * i[:, None] * (i[None, :] + 0.25) / outer
    twist = 2.0 * np.pi * j[None, :] * (i[:, None] + 0.25) / length
    second = 2.0 * np.pi * (j[:, None] * j[None, :] % inner) / inner
    cos, sin = np.cos(second), np.sin(second)
    packed = np.zeros((inner + 5 * outer, 2 * inner))
    packed[:inner] = np.concatenate([cos, sin], 1)
    packed[inner:inner + outer] = np.concatenate([np.cos(twist), np.sin(twist)], 1)
    packed[inner + outer:inner + 3 * outer, :outer] = np.concatenate([np.cos(first).T, -np.sin(first).T], 0)
    back = np.concatenate([np.cos(first), -np.sin(first)], 1) / length
    packed[inner + 3 * outer:inner + 4 * outer, :2 * outer] = back
    packed[inner + 4 * outer:, :2 * outer] = back[i.reshape(nx, nz, 2).transpose(1, 0, 2).reshape(-1)]
    return packed.astype(np.float32)


def halves(table):
    high = table.astype(BF16)
    return high, (table - high.astype(F32)).astype(BF16)


def split_wide(real, imag):
    wide = jnp.concatenate([real, imag], axis=1)
    high = wide.astype(BF16)
    low = (wide - high.astype(F32)).astype(BF16)
    return jnp.concatenate([high, low, high], axis=1)


def dot(a, b):
    return jnp.dot(a, b, preferred_element_type=F32)


def kernel(
    sizes,
    q_hbm, k_hbm, v_hbm, f_hbm, w_hbm, go_hbm, table_hbm,
    out_ref, gq_ref, gk_ref, gv_ref, gf_ref, gw_ref,
    q_ref, k_ref, v_ref, f_ref, go_ref, table,
    fo_ref, fi_ref, bi_ref, bo_ref, bz_ref, w_ref,
    send_a, recv_a, send_b, recv_b, send_c, recv_c, send_d, recv_d,
    wide, spec_g, spec_f, spec_h, zbuf, full, full_t, q_t, q_send, q_recv,
    conv_send, conv_recv, mix_send, mix_recv, grad_recv, part_send, part_recv,
    out_send, out_recv, out_own, gm_t,
    load_sem, send_sem, recv_sem,
):
    nx, nz, ns, ny, rows, scale = sizes
    me = lax.axis_index("seq")
    my = lax.axis_index("ch")
    my_x, my_z, my_k = me // (2 * nz), me // 2 % nz, me % 2
    group = nx * 2
    place = my_x * 2 + my_k
    half = nz // 2
    chans = ns * 8
    width = go_ref.shape[1]
    cut = width // (2 * nz)

    def peer(step):
        return lax.rem(me + step * 53, ns)

    def run_of(device):
        x, z, k = device // (2 * nz), device // 2 % nz, device % 2
        return ((z // half * 2 + k) * nx + x) * half + z % half

    def seq_of(x, z, k):
        return (x * nz + z) * 2 + k

    def remote(src, dst, index, to):
        return pltpu.make_async_remote_copy(
            src_ref=src, dst_ref=dst, send_sem=send_sem.at[index], recv_sem=recv_sem.at[index],
            device_id=to, device_id_type=MESH,
        )

    def nearby(index, ref, count):
        part = ref.at[pl.ds(0, count)]
        return remote(part, part, index, {"seq": peer(1)})

    loads = [
        pltpu.make_async_copy(src, dst, load_sem.at[i])
        for i, (src, dst) in enumerate((
            (k_hbm, k_ref), (v_hbm, v_ref), (f_hbm, f_ref), (go_hbm, go_ref),
            (table_hbm, table), (q_hbm, q_ref), (w_hbm, w_ref),
        ))
    ]
    for load in loads:
        load.start()

    barrier = pltpu.get_barrier_semaphore()

    def greet(step, carry):
        pl.semaphore_signal(barrier, inc=1, device_id={"seq": peer(step)}, device_id_type=MESH)
        return carry

    lax.fori_loop(1, ns, greet, 0)
    for step in range(1, ny):
        pl.semaphore_signal(barrier, inc=1, device_id={"ch": lax.rem(my + step, ny)}, device_id_type=MESH)

    for load in loads[:3]:
        load.wait()
    gated = k_ref[...].astype(F32) * v_ref[...].astype(F32)
    gated_t = gated.T.reshape(ns, 8, rows)
    taps_t = f_ref[...].astype(F32).T.reshape(ns, 8, rows)
    send_a[...] = jnp.concatenate([gated_t, taps_t], axis=1).astype(BF16)
    recv_a[me] = send_a[run_of(me)]
    loads[3].wait()
    pl.semaphore_wait(barrier, ns - 1 + ny - 1)

    def exchange(send, recv, index, where, there):
        def start(step, carry):
            other = peer(step)
            remote(where(send, other), there(recv, me), index, {"seq": other}).start()
            return carry

        lax.fori_loop(1, ns, start, 0)

    def slot(ref, i):
        return ref.at[i]

    def eight(ref, i):
        return ref.at[pl.ds(pl.multiple_of(i * 8, 8), 8)]

    pieces = half
    lows = [*range(0, half, 2), *range(1, half, 2)]
    moved_full = []
    moved_grad = []

    def send_piece(p):
        for u in range(2):
            first = (u * half + lows[p]) * 2 * cut
            full[p, my, :, u * 2 * cut:(u + 1) * 2 * cut] = go_ref[:, first:first + 2 * cut]
        for step in (1, ny - 1, *range(2, ny - 1))[:ny - 1]:
            remote(full.at[p, my], full.at[p, my], 1 + p, {"ch": lax.rem(my + step, ny)}).start()
        moved_full.append(nearby(1 + p, full.at[p], ny - 1))

    for p in range(pieces):
        send_piece(p)
    exchange(send_a, recv_a, 0, lambda ref, d: slot(ref, run_of(d)), slot)
    moved_a = nearby(0, recv_a, ns - 1)

    def members():
        for step in range(1, group):
            other = lax.rem(place + step, group)
            yield other, {"seq": seq_of(other // 2, my_z, other % 2)}

    loads[5].wait()
    q_t[...] = q_ref[...].astype(F32).T
    q_send[...] = q_t[...].astype(BF16).reshape(q_send.shape)
    for other, to in members():
        remote(q_send.at[:, other % 2, other // 2], q_recv.at[place], 9, to).start()
    moved_q = nearby(9, q_recv, group - 1)
    q_recv[place] = q_send[:, my_k, my_x]

    def turn_over(p):
        moved_full[p].wait_recv()
        for j in range(ny):
            full_t[j, :, lows[p]] = full[p, j].T.reshape(2, 2, cut, rows)

    def pass_on(p):
        low = lows[p]
        for step in range(1, nx):
            j = lax.rem(my_x + step, nx)
            remote(
                full_t.at[j, :, low], grad_recv.at[my_k, my_x, :, low], 5 + p, {"seq": seq_of(j, my_z, my_k)}
            ).start()
        grad_recv[my_k, my_x, :, low] = full_t[my_x, :, low]
        got = grad_recv.at[0, pl.ds(0, nx - 1), :, low]
        moved_grad.append(remote(got, got, 5 + p, {"seq": peer(1)}))

    loads[4].wait()
    cos, sin = table[:rows, :rows], table[:rows, rows:]
    high, low = halves(table[rows + ns:rows + 3 * ns, :ns])
    fo_ref[...] = jnp.concatenate([high, low], axis=1)
    high, low = halves(jnp.concatenate([jnp.concatenate([cos, -sin], 1), jnp.concatenate([sin, cos], 1)], 0))
    fi_ref[...] = jnp.concatenate([high, high, low], axis=0)
    high, low = halves(jnp.concatenate([jnp.concatenate([cos, sin], 1), jnp.concatenate([-sin, cos], 1)], 0))
    bi_ref[...] = jnp.concatenate([high, high, low], axis=0)
    high, low = halves(table[rows + 3 * ns:rows + 4 * ns, :2 * ns])
    bo_ref[...] = jnp.concatenate([high, high, low], axis=1)
    high, low = halves(table[rows + 4 * ns:, :2 * ns])
    bz_ref[...] = jnp.concatenate([high, high, low], axis=1)
    turn = pl.ds(rows, ns)

    def spectra(src, count, base, spec):
        for s in range(0, 8, 2):
            pair = [src[pl.ds(base + s + u, ns, stride=count), :] for u in range(2)]
            block = jnp.concatenate(pair, axis=1).astype(BF16)
            stage = dot(fo_ref[...], jnp.concatenate([block, block], axis=0))
            for u in range(2):
                re = stage[:ns, u * rows:(u + 1) * rows]
                im = stage[ns:, u * rows:(u + 1) * rows]
                cos, sin = table[turn, :rows], table[turn, rows:]
                zbuf[pl.ds((s + u) * ns, ns), :] = split_wide(re * cos + im * sin, im * cos - re * sin)
        spec[...] = dot(zbuf[...], fi_ref[...])

    def inverse(left, right, conj, last, dst, count, base):
        n = rows
        for s in range(8):
            part = pl.ds(s * ns, ns)
            lr, li = left[part, :n], left[part, n:]
            rr, ri = right[part, :n], right[part, n:]
            if conj:
                zbuf[part, :] = split_wide(lr * rr + li * ri, li * rr - lr * ri)
            else:
                zbuf[part, :] = split_wide(lr * rr - li * ri, li * rr + lr * ri)
        full_stage = dot(zbuf[...], bi_ref[...])
        for s in range(0, 8, 2):
            cols = []
            for u in range(2):
                re = full_stage[(s + u) * ns:(s + u + 1) * ns, :n]
                im = full_stage[(s + u) * ns:(s + u + 1) * ns, n:]
                cos, sin = table[turn, :rows], table[turn, rows:]
                turned = jnp.concatenate([re * cos - im * sin, im * cos + re * sin], axis=0)
                high = turned.astype(BF16)
                low = (turned - high.astype(F32)).astype(BF16)
                cols.append(jnp.concatenate([high, low, high], axis=0))
            back = dot(last[...], jnp.concatenate(cols, axis=1))
            for u in range(2):
                dst[pl.ds(base + s + u, ns, stride=count), :] = back[:, u * n:(u + 1) * n]

    turn_over(0)
    pass_on(0)
    moved_a.wait_recv()
    wide[...] = recv_a[...].astype(F32).reshape(ns * 16, rows)
    spectra(wide, 16, 0, spec_g)
    spectra(wide, 16, 8, spec_f)
    inverse(spec_g, spec_f, False, bz_ref, send_c, 8, 0)
    send_b[...] = send_c[...].astype(BF16).reshape(nz, group * 8, rows)
    for step in range(1, nz):
        other = lax.rem(my_z + step, nz)
        remote(send_b.at[other], recv_b.at[my_z], 10, {"seq": seq_of(my_x, other, my_k)}).start()
    moved_b = nearby(10, recv_b, nz - 1)
    recv_b[my_z] = send_b[my_z]

    loads[6].wait()

    def add_up(p):
        total = jnp.zeros((chans, rows), F32) if p == 0 else gm_t[...]
        for j in range(ny):
            first = [j * width + (u * half + lows[p]) * 2 * cut for u in range(2)]
            weights = jnp.concatenate([w_ref[:, i:i + 2 * cut] for i in first], axis=1)
            total += dot(weights, full_t[j, :, lows[p]].reshape(4 * cut, rows))
        gm_t[...] = total

    add_up(0)
    for p in range(1, pieces - 1):
        turn_over(p)
        pass_on(p)
        add_up(p)

    moved_q.wait_recv()
    moved_b.wait_recv()
    conv = recv_b[...].astype(F32).reshape(nz, group, 8, rows)
    conv = jnp.swapaxes(conv, 0, 1).reshape(group, 2, half * 8, rows)
    mixed = (q_recv[...].astype(F32) * conv).astype(BF16)
    mix_send[...] = jnp.swapaxes(mixed, 0, 1)
    conv_send[...] = conv.astype(BF16)
    for other, to in members():
        remote(conv_send.at[other], conv_recv.at[:, my_k, my_x], 13, to).start()
    moved_conv = nearby(13, conv_send, group - 1)
    conv_recv[:, my_k, my_x] = conv_send[place]

    turn_over(pieces - 1)
    pass_on(pieces - 1)
    add_up(pieces - 1)

    send_c[...] = (gm_t[...] * q_t[...]).astype(BF16).astype(F32)
    eight(recv_c, me)[...] = eight(send_c, run_of(me))[...]
    exchange(send_c, recv_c, 14, lambda ref, d: eight(ref, run_of(d)), eight)
    moved_c = nearby(14, recv_c, 8 * (ns - 1))

    for step in range(1, nx):
        other = lax.rem(my_x + step, nx)
        remote(mix_send, mix_recv.at[my_x], 11, {"seq": seq_of(other, my_z, my_k)}).start()
    moved_mix = nearby(11, mix_recv, nx - 1)
    mix_recv[my_x] = mix_send[...]
    def swap(h):
        for p in range(h * half // 2, (h + 1) * half // 2):
            moved_grad[p].wait_recv()
            mine = grad_recv.at[my_k, :, :, lows[p]]
            remote(mine, mine, 16 + h, {"seq": seq_of(my_x, my_z, 1 - my_k)}).start()
        both = grad_recv.at[0, :, :, pl.ds(0, half // 2)]
        return remote(both, both, 16 + h, {"seq": peer(1)})

    moved_swap = [swap(0), swap(1)]


    moved_conv.wait_recv()
    conv = conv_recv[...].astype(F32).reshape(chans, rows)
    gq_ref[...] = (gm_t[...] * conv).T.astype(BF16)
    mixed = (q_t[...] * conv).T.astype(BF16)
    for step in range(1, ny):
        other = lax.rem(my + step, ny)
        columns = pl.ds(pl.multiple_of(other * width, width), width)
        out_send[other] = dot(mixed, w_ref[:, columns]).astype(BF16)
        remote(out_send.at[other], out_recv.at[my], 15, {"ch": other}).start()
    moved_out = nearby(15, out_recv, ny - 1)
    out_own[...] = dot(mixed, w_ref[:, pl.ds(pl.multiple_of(my * width, width), width)])

    moved_c.wait_recv()
    spectra(recv_c, 8, 0, spec_h)
    inverse(spec_h, spec_f, True, bo_ref, wide, 16, 0)
    inverse(spec_h, spec_g, True, bo_ref, wide, 16, 8)
    send_d[...] = wide[...].reshape(ns, 16, rows).astype(BF16)
    recv_d[run_of(me)] = send_d[me]
    exchange(send_d, recv_d, 20, slot, lambda ref, d: slot(ref, run_of(d)))
    moved_d = nearby(20, recv_d, ns - 1)

    moved_mix.wait_recv()
    right = jnp.concatenate(
        [mix_recv[:, p, i].reshape(half * 8 * nx, rows) for p in range(2) for i in range(group)], axis=1
    )
    right = jnp.concatenate([right[:, :group * rows], right[:, group * rows:]], axis=0)
    here = my_z * 2 + my_k
    for h in range(2):
        moved_swap[h].wait_recv()
        for t in (half // 2, *(i for i in range(1, half) if i != half // 2), 0):
            z = lax.rem(2 * (my_z // 2 + t), nz) + h
            left = jnp.concatenate(
                [grad_recv[i % 2, i // 2, z // half, z % half].reshape(2 * cut, rows) for i in range(group)], axis=1
            )
            part = lax.dot_general(left, right, (((1,), (1,)), ((), ())), preferred_element_type=F32)
            part_send[z] = part.astype(BF16).reshape(2, cut, half * 16 * nx)
            for k in range(2):
                there = z * 2 + k

                @pl.when(there == here)
                def _():
                    part_recv[here] = part_send[z, k]

                @pl.when(there != here)
                def _():
                    remote(
                        part_send.at[z, k], part_recv.at[here], 18, {"seq": my_x * 2 * nz + there}
                    ).start()
    moved_part = nearby(18, part_recv, 2 * nz - 1)

    moved_out.wait_recv()
    total = out_own[...]
    for step in range(1, ny):
        total += out_recv[lax.rem(my + step, ny)].astype(F32)
    out_ref[...] = total.astype(BF16)

    moved_d.wait_recv()
    back = recv_d[...].astype(F32)
    gg = back[:, :8].reshape(chans, rows).T
    gk_ref[...] = (gg * v_ref[...].astype(F32)).astype(BF16)
    gv_ref[...] = (gg * k_ref[...].astype(F32)).astype(BF16)
    gf_ref[...] = back[:, 8:].reshape(chans, rows).T * scale

    moved_part.wait_recv()
    lanes = half * 8 * nx
    for k in range(2):
        weight = part_recv[k].astype(F32)
        for i in range(1, nz):
            weight += part_recv[2 * i + k].astype(F32)
        for p in range(2):
            gw_ref[:, (2 * p + k) * lanes:(2 * p + k + 1) * lanes] = weight[:, p * lanes:(p + 1) * lanes] * scale

    for moved in (
        moved_a, moved_b, moved_c, moved_d, moved_q, moved_conv, moved_out,
        *moved_full, moved_mix, moved_part, *moved_grad, *moved_swap,
    ):
        moved.wait_send()


def store(*refs):
    count = len(refs) // 2
    copies = [pltpu.make_async_copy(refs[i], refs[count + i], refs[-1].at[i]) for i in range(count)]
    for copy in copies:
        copy.start()
    for copy in copies:
        copy.wait()


def solution(mesh):
    ns, ny = mesh.shape["seq"], mesh.shape["ch"]
    nx, nz, _ = GRID[ns]

    def shards(q, k, v, f, w, g):
        rows, chans = q.shape
        width = g.shape[1]
        cut = width // (2 * nz)
        group = nx * 2
        run = nz * 4
        pieces = nz // 2
        table = tables(ns, rows, nx, nz)
        vm = pltpu.VMEM
        sizes = (nx, nz, ns, ny, rows, (ns * rows) ** -0.5)
        tok = lambda dtype: jax.ShapeDtypeStruct((rows, chans), dtype)
        results = pl.pallas_call(
            functools.partial(kernel, sizes),
            out_shape=(
                jax.ShapeDtypeStruct((rows, width), BF16), tok(BF16), tok(BF16), tok(BF16), tok(F32),
                jax.ShapeDtypeStruct((cut, chans), F32),
            ),
            in_specs=[pl.BlockSpec(memory_space=pl.ANY)] * 7,
            out_specs=(pl.BlockSpec(memory_space=pltpu.VMEM),) * 6,
            scratch_shapes=[
                vm(q.shape, BF16), vm(q.shape, BF16), vm(q.shape, BF16), vm(q.shape, BF16),
                vm(g.shape, BF16), vm(table.shape, F32),
                vm((2 * ns, 2 * ns), BF16), vm((6 * rows, 2 * rows), BF16), vm((6 * rows, 2 * rows), BF16),
                vm((ns, 6 * ns), BF16), vm((ns, 6 * ns), BF16), vm(w.shape, BF16),
                vm((ns, 16, rows), BF16), vm((ns, 16, rows), BF16),
                vm((nz, group * 8, rows), BF16), vm((nz, group * 8, rows), BF16),
                vm((chans, rows), F32), vm((chans, rows), F32),
                vm((ns, 16, rows), BF16), vm((ns, 16, rows), BF16),
                vm((ns * 16, rows), F32),
                vm((chans, 2 * rows), F32), vm((chans, 2 * rows), F32), vm((chans, 2 * rows), F32),
                vm((chans, 6 * rows), BF16),
                vm((pieces, ny, rows, width // pieces), BF16), vm((ny, 2, nz // 2, 2, cut, rows), BF16),
                vm((chans, rows), F32),
                vm((2, 2, nx, run, rows), BF16), vm((group, 2, run, rows), BF16),
                vm((group, 2, run, rows), BF16), vm((2, 2, nx, run, rows), BF16),
                vm((2, group, run, rows), BF16), vm((nx, 2, group, run, rows), BF16),
                vm((2, nx, 2, nz // 2, 2, cut, rows), BF16),
                vm((nz, 2, cut, 2 * run * nx), BF16), vm((2 * nz, cut, 2 * run * nx), BF16),
                vm((ny, rows, width), BF16), vm((ny, rows, width), BF16), vm((rows, width), F32),
                vm((chans, rows), F32),
                pltpu.SemaphoreType.DMA((7,)), pltpu.SemaphoreType.DMA((21,)), pltpu.SemaphoreType.DMA((21,)),
            ],
            compiler_params=pltpu.CompilerParams(
                collective_id=0, has_side_effects=True, vmem_limit_bytes=56 * 1024 * 1024
            ),
        )(q, k, v, f, w, g, table)
        *rest, gw = pl.pallas_call(
            store,
            out_shape=tuple(jax.ShapeDtypeStruct(r.shape, r.dtype) for r in results),
            in_specs=[pl.BlockSpec(memory_space=pltpu.VMEM)] * 6,
            out_specs=(pl.BlockSpec(memory_space=pl.ANY),) * 6,
            scratch_shapes=[pltpu.SemaphoreType.DMA((6,))],
        )(*results)
        return (*rest, gw.T)

    tokens = P("seq", "ch")
    return jax.shard_map(
        shards,
        mesh=mesh,
        in_specs=(tokens, tokens, tokens, tokens, P("ch", None), tokens),
        out_specs=(tokens, tokens, tokens, tokens, tokens, P("ch", "seq")),
        check_vma=False,
    )
```

```python
import functools

import jax
import jax.numpy as jnp
import numpy as np
from jax import lax
from jax.experimental import pallas as pl
from jax.experimental.pallas import tpu as pltpu
from jax.sharding import PartitionSpec as P

F32 = jnp.float32
BF16 = jnp.bfloat16
MESH = pl.DeviceIdType.MESH
GRID = {64: (4, 8, 2), 16: (2, 4, 2)}


def tables(outer, inner, nx, nz):
    length = outer * inner
    i = np.arange(outer)
    j = np.arange(inner)
    first = 2.0 * np.pi * i[:, None] * (i[None, :] + 0.25) / outer
    twist = 2.0 * np.pi * j[None, :] * (i[:, None] + 0.25) / length
    second = 2.0 * np.pi * (j[:, None] * j[None, :] % inner) / inner
    cos, sin = np.cos(second), np.sin(second)
    packed = np.zeros((inner + 5 * outer, 2 * inner))
    packed[:inner] = np.concatenate([cos, sin], 1)
    packed[inner:inner + outer] = np.concatenate([np.cos(twist), np.sin(twist)], 1)
    packed[inner + outer:inner + 3 * outer, :outer] = np.concatenate([np.cos(first).T, -np.sin(first).T], 0)
    back = np.concatenate([np.cos(first), -np.sin(first)], 1) / length
    packed[inner + 3 * outer:inner + 4 * outer, :2 * outer] = back
    packed[inner + 4 * outer:, :2 * outer] = back[i.reshape(nx, nz, 2).transpose(1, 0, 2).reshape(-1)]
    return packed.astype(np.float32)


def halves(table):
    high = table.astype(BF16)
    return high, (table - high.astype(F32)).astype(BF16)


def split_wide(real, imag):
    wide = jnp.concatenate([real, imag], axis=1)
    high = wide.astype(BF16)
    low = (wide - high.astype(F32)).astype(BF16)
    return jnp.concatenate([high, low, high], axis=1)


def dot(a, b):
    return jnp.dot(a, b, preferred_element_type=F32)


def kernel(
    sizes,
    q_hbm, k_hbm, v_hbm, f_hbm, w_hbm, go_hbm, table_hbm,
    out_ref, gq_ref, gk_ref, gv_ref, gf_ref, gw_ref,
    q_ref, k_ref, v_ref, f_ref, go_ref, table,
    fo_ref, fi_ref, bi_ref, bo_ref, bz_ref, w_ref,
    send_a, recv_a, send_b, recv_b, stage_c, send_c, recv_c, give_c, take_c, send_d, recv_d,
    wide, spec_g, spec_f, spec_h, zbuf, full, full_t, q_t, q_send, q_recv,
    conv_send, conv_recv, mix_send, mix_recv, grad_recv, part_send, part_recv,
    out_send, out_recv, out_own, gm_t,
    load_sem, send_sem, recv_sem,
):
    nx, nz, ns, ny, rows, scale = sizes
    me = lax.axis_index("seq")
    my = lax.axis_index("ch")
    my_x, my_z, my_k = me // (2 * nz), me // 2 % nz, me % 2
    group = nx * 2
    place = my_x * 2 + my_k
    half = nz // 2
    chans = ns * 8
    width = go_ref.shape[1]
    cut = width // (2 * nz)

    def peer(step):
        return lax.rem(me + step * 53, ns)

    def run_of(device):
        x, z, k = device // (2 * nz), device // 2 % nz, device % 2
        return ((z // half * 2 + k) * nx + x) * half + z % half

    def seq_of(x, z, k):
        return (x * nz + z) * 2 + k

    def remote(src, dst, index, to):
        return pltpu.make_async_remote_copy(
            src_ref=src, dst_ref=dst, send_sem=send_sem.at[index], recv_sem=recv_sem.at[index],
            device_id=to, device_id_type=MESH,
        )

    def nearby(index, ref, count):
        part = ref.at[pl.ds(0, count)]
        return remote(part, part, index, {"seq": peer(1)})

    loads = [
        pltpu.make_async_copy(src, dst, load_sem.at[i])
        for i, (src, dst) in enumerate((
            (k_hbm, k_ref), (v_hbm, v_ref), (f_hbm, f_ref), (go_hbm, go_ref),
            (table_hbm, table), (q_hbm, q_ref), (w_hbm, w_ref),
        ))
    ]
    for load in loads:
        load.start()

    barrier = pltpu.get_barrier_semaphore()

    def greet(step, carry):
        pl.semaphore_signal(barrier, inc=1, device_id={"seq": peer(step)}, device_id_type=MESH)
        return carry

    lax.fori_loop(1, ns, greet, 0)
    for step in range(1, ny):
        pl.semaphore_signal(barrier, inc=1, device_id={"ch": lax.rem(my + step, ny)}, device_id_type=MESH)

    for load in loads[:3]:
        load.wait()
    gated = k_ref[...].astype(F32) * v_ref[...].astype(F32)
    gated_t = gated.T.reshape(ns, 8, rows)
    taps_t = f_ref[...].astype(F32).T.reshape(ns, 8, rows)
    send_a[...] = jnp.concatenate([gated_t, taps_t], axis=1).astype(BF16)
    recv_a[me] = send_a[run_of(me)]
    loads[3].wait()
    pl.semaphore_wait(barrier, ns - 1 + ny - 1)

    def exchange(send, recv, index, where, there):
        def start(step, carry):
            other = peer(step)
            remote(where(send, other), there(recv, me), index, {"seq": other}).start()
            return carry

        lax.fori_loop(1, ns, start, 0)

    def slot(ref, i):
        return ref.at[i]

    pieces = half
    lows = [*range(0, half, 2), *range(1, half, 2)]
    moved_full = []
    moved_grad = []

    def send_piece(p):
        for u in range(2):
            first = (u * half + lows[p]) * 2 * cut
            full[p, my, :, u * 2 * cut:(u + 1) * 2 * cut] = go_ref[:, first:first + 2 * cut]
        for step in (1, ny - 1, *range(2, ny - 1))[:ny - 1]:
            remote(full.at[p, my], full.at[p, my], 1 + p, {"ch": lax.rem(my + step, ny)}).start()
        moved_full.append(nearby(1 + p, full.at[p], ny - 1))

    for p in range(pieces):
        send_piece(p)
    exchange(send_a, recv_a, 0, lambda ref, d: slot(ref, run_of(d)), slot)
    moved_a = nearby(0, recv_a, ns - 1)

    def members():
        for step in range(1, group):
            other = lax.rem(place + step, group)
            yield other, {"seq": seq_of(other // 2, my_z, other % 2)}

    loads[5].wait()
    q_t[...] = q_ref[...].astype(F32).T
    q_send[...] = q_t[...].astype(BF16).reshape(q_send.shape)
    for other, to in members():
        remote(q_send.at[:, other % 2, other // 2], q_recv.at[place], 9, to).start()
    moved_q = nearby(9, q_recv, group - 1)
    q_recv[place] = q_send[:, my_k, my_x]

    def turn_over(p):
        moved_full[p].wait_recv()
        for j in range(ny):
            full_t[j, :, lows[p]] = full[p, j].T.reshape(2, 2, cut, rows)

    def pass_on(p):
        low = lows[p]
        for step in range(1, nx):
            j = lax.rem(my_x + step, nx)
            remote(
                full_t.at[j, :, low], grad_recv.at[my_k, my_x, :, low], 5 + p, {"seq": seq_of(j, my_z, my_k)}
            ).start()
        grad_recv[my_k, my_x, :, low] = full_t[my_x, :, low]
        got = grad_recv.at[0, pl.ds(0, nx - 1), :, low]
        moved_grad.append(remote(got, got, 5 + p, {"seq": peer(1)}))

    loads[4].wait()
    cos, sin = table[:rows, :rows], table[:rows, rows:]
    high, low = halves(table[rows + ns:rows + 3 * ns, :ns])
    fo_ref[...] = jnp.concatenate([high, low], axis=1)
    high, low = halves(jnp.concatenate([jnp.concatenate([cos, -sin], 1), jnp.concatenate([sin, cos], 1)], 0))
    fi_ref[...] = jnp.concatenate([high, high, low], axis=0)
    high, low = halves(jnp.concatenate([jnp.concatenate([cos, sin], 1), jnp.concatenate([-sin, cos], 1)], 0))
    bi_ref[...] = jnp.concatenate([high, high, low], axis=0)
    high, low = halves(table[rows + 3 * ns:rows + 4 * ns, :2 * ns])
    bo_ref[...] = jnp.concatenate([high, high, low], axis=1)
    high, low = halves(table[rows + 4 * ns:, :2 * ns])
    bz_ref[...] = jnp.concatenate([high, high, low], axis=1)
    turn = pl.ds(rows, ns)

    def spectra(src, count, base, spec):
        for s in range(0, 8, 2):
            pair = [src[pl.ds(base + s + u, ns, stride=count), :] for u in range(2)]
            block = jnp.concatenate(pair, axis=1).astype(BF16)
            stage = dot(fo_ref[...], jnp.concatenate([block, block], axis=0))
            for u in range(2):
                re = stage[:ns, u * rows:(u + 1) * rows]
                im = stage[ns:, u * rows:(u + 1) * rows]
                cos, sin = table[turn, :rows], table[turn, rows:]
                zbuf[pl.ds((s + u) * ns, ns), :] = split_wide(re * cos + im * sin, im * cos - re * sin)
        spec[...] = dot(zbuf[...], fi_ref[...])

    def inverse(left, right, conj, last, dst, count, base):
        n = rows
        for s in range(8):
            part = pl.ds(s * ns, ns)
            lr, li = left[part, :n], left[part, n:]
            rr, ri = right[part, :n], right[part, n:]
            if conj:
                zbuf[part, :] = split_wide(lr * rr + li * ri, li * rr - lr * ri)
            else:
                zbuf[part, :] = split_wide(lr * rr - li * ri, li * rr + lr * ri)
        full_stage = dot(zbuf[...], bi_ref[...])
        for s in range(0, 8, 2):
            cols = []
            for u in range(2):
                re = full_stage[(s + u) * ns:(s + u + 1) * ns, :n]
                im = full_stage[(s + u) * ns:(s + u + 1) * ns, n:]
                cos, sin = table[turn, :rows], table[turn, rows:]
                turned = jnp.concatenate([re * cos - im * sin, im * cos + re * sin], axis=0)
                high = turned.astype(BF16)
                low = (turned - high.astype(F32)).astype(BF16)
                cols.append(jnp.concatenate([high, low, high], axis=0))
            back = dot(last[...], jnp.concatenate(cols, axis=1))
            for u in range(2):
                dst[pl.ds(base + s + u, ns, stride=count), :] = back[:, u * n:(u + 1) * n]

    turn_over(0)
    pass_on(0)
    moved_a.wait_recv()
    wide[...] = recv_a[...].astype(F32).reshape(ns * 16, rows)
    spectra(wide, 16, 0, spec_g)
    spectra(wide, 16, 8, spec_f)
    inverse(spec_g, spec_f, False, bz_ref, stage_c, 8, 0)
    send_b[...] = stage_c[...].astype(BF16).reshape(nz, group * 8, rows)
    for step in range(1, nz):
        other = lax.rem(my_z + step, nz)
        remote(send_b.at[other], recv_b.at[my_z], 10, {"seq": seq_of(my_x, other, my_k)}).start()
    moved_b = nearby(10, recv_b, nz - 1)
    recv_b[my_z] = send_b[my_z]

    loads[6].wait()

    def add_up(p):
        total = jnp.zeros((chans, rows), F32) if p == 0 else gm_t[...]
        for j in range(ny):
            first = [j * width + (u * half + lows[p]) * 2 * cut for u in range(2)]
            weights = jnp.concatenate([w_ref[:, i:i + 2 * cut] for i in first], axis=1)
            total += dot(weights, full_t[j, :, lows[p]].reshape(4 * cut, rows))
        gm_t[...] = total

    add_up(0)
    for p in range(1, pieces - 1):
        turn_over(p)
        pass_on(p)
        add_up(p)

    moved_q.wait_recv()
    moved_b.wait_recv()
    conv = recv_b[...].astype(F32).reshape(nz, group, 8, rows)
    conv = jnp.swapaxes(conv, 0, 1).reshape(group, 2, half * 8, rows)
    mixed = (q_recv[...].astype(F32) * conv).astype(BF16)
    mix_send[...] = jnp.swapaxes(mixed, 0, 1)
    conv_send[...] = conv.astype(BF16)
    for other, to in members():
        remote(conv_send.at[other], conv_recv.at[:, my_k, my_x], 13, to).start()
    moved_conv = nearby(13, conv_send, group - 1)
    conv_recv[:, my_k, my_x] = conv_send[place]

    turn_over(pieces - 1)
    pass_on(pieces - 1)
    add_up(pieces - 1)

    grad_conv = (gm_t[...] * q_t[...]).reshape(2, 2, nx, half, 8, rows)
    send_c[...] = jnp.transpose(grad_conv, (2, 0, 3, 1, 4, 5)).reshape(ns // 2, 16, rows).astype(BF16)
    chip = me // 2

    def start_c(step, carry):
        other = lax.rem(chip + step * 11, ns // 2)
        remote(send_c.at[other], recv_c.at[chip], 14, {"seq": other * 2 + my_k}).start()
        return carry

    lax.fori_loop(1, ns // 2, start_c, 0)
    recv_c[chip] = send_c[chip]
    moved_c = nearby(14, recv_c, ns // 2 - 1)

    for step in range(1, nx):
        other = lax.rem(my_x + step, nx)
        remote(mix_send, mix_recv.at[my_x], 11, {"seq": seq_of(other, my_z, my_k)}).start()
    moved_mix = nearby(11, mix_recv, nx - 1)
    mix_recv[my_x] = mix_send[...]
    def swap(h):
        for p in range(h * half // 2, (h + 1) * half // 2):
            moved_grad[p].wait_recv()
            mine = grad_recv.at[my_k, :, :, lows[p]]
            remote(mine, mine, 16 + h, {"seq": seq_of(my_x, my_z, 1 - my_k)}).start()
        both = grad_recv.at[0, :, :, pl.ds(0, half // 2)]
        return remote(both, both, 16 + h, {"seq": peer(1)})

    moved_swap = [swap(0), swap(1)]


    moved_conv.wait_recv()
    conv = conv_recv[...].astype(F32).reshape(chans, rows)
    gq_ref[...] = (gm_t[...] * conv).T.astype(BF16)
    mixed = (q_t[...] * conv).T.astype(BF16)
    for step in range(1, ny):
        other = lax.rem(my + step, ny)
        columns = pl.ds(pl.multiple_of(other * width, width), width)
        out_send[other] = dot(mixed, w_ref[:, columns]).astype(BF16)
        remote(out_send.at[other], out_recv.at[my], 15, {"ch": other}).start()
    moved_out = nearby(15, out_recv, ny - 1)
    out_own[...] = dot(mixed, w_ref[:, pl.ds(pl.multiple_of(my * width, width), width)])

    moved_c.wait_recv()
    got = recv_c[...].astype(F32)
    keep = jnp.where(my_k == 0, got[:, :8], got[:, 8:])
    give = jnp.where(my_k == 0, got[:, 8:], got[:, :8])
    give_c[...] = give.reshape(ns // 4, 16, rows).astype(BF16)
    moved_give = remote(give_c, take_c, 12, {"seq": seq_of(my_x, my_z, 1 - my_k)})
    moved_give.start()
    moved_give.wait_recv()
    take = take_c[...].astype(F32).reshape(ns // 2, 8, rows)
    both = [jnp.where(my_k == 0, keep, take), jnp.where(my_k == 0, take, keep)]
    wide[pl.ds(0, ns * 8), :] = jnp.stack(both, axis=1).reshape(ns * 8, rows)
    spectra(wide, 8, 0, spec_h)
    inverse(spec_h, spec_f, True, bo_ref, wide, 16, 0)
    inverse(spec_h, spec_g, True, bo_ref, wide, 16, 8)
    send_d[...] = wide[...].reshape(ns, 16, rows).astype(BF16)
    recv_d[run_of(me)] = send_d[me]
    exchange(send_d, recv_d, 20, slot, lambda ref, d: slot(ref, run_of(d)))
    moved_d = nearby(20, recv_d, ns - 1)

    moved_mix.wait_recv()
    right = jnp.concatenate(
        [mix_recv[:, p, i].reshape(half * 8 * nx, rows) for p in range(2) for i in range(group)], axis=1
    )
    right = jnp.concatenate([right[:, :group * rows], right[:, group * rows:]], axis=0)
    here = my_z * 2 + my_k
    for h in range(2):
        moved_swap[h].wait_recv()
        for t in (half // 2, *(i for i in range(1, half) if i != half // 2), 0):
            z = lax.rem(2 * (my_z // 2 + t), nz) + h
            left = jnp.concatenate(
                [grad_recv[i % 2, i // 2, z // half, z % half].reshape(2 * cut, rows) for i in range(group)], axis=1
            )
            part = lax.dot_general(left, right, (((1,), (1,)), ((), ())), preferred_element_type=F32)
            part_send[z] = part.astype(BF16).reshape(2, cut, half * 16 * nx)
            for k in range(2):
                there = z * 2 + k

                @pl.when(there == here)
                def _():
                    part_recv[here] = part_send[z, k]

                @pl.when(there != here)
                def _():
                    remote(
                        part_send.at[z, k], part_recv.at[here], 18, {"seq": my_x * 2 * nz + there}
                    ).start()
    moved_part = nearby(18, part_recv, 2 * nz - 1)

    moved_out.wait_recv()
    total = out_own[...]
    for step in range(1, ny):
        total += out_recv[lax.rem(my + step, ny)].astype(F32)
    out_ref[...] = total.astype(BF16)

    moved_d.wait_recv()
    back = recv_d[...].astype(F32)
    gg = back[:, :8].reshape(chans, rows).T
    gk_ref[...] = (gg * v_ref[...].astype(F32)).astype(BF16)
    gv_ref[...] = (gg * k_ref[...].astype(F32)).astype(BF16)
    gf_ref[...] = back[:, 8:].reshape(chans, rows).T * scale

    moved_part.wait_recv()
    lanes = half * 8 * nx
    for k in range(2):
        weight = part_recv[k].astype(F32)
        for i in range(1, nz):
            weight += part_recv[2 * i + k].astype(F32)
        for p in range(2):
            gw_ref[:, (2 * p + k) * lanes:(2 * p + k + 1) * lanes] = weight[:, p * lanes:(p + 1) * lanes] * scale

    for moved in (
        moved_a, moved_b, moved_c, moved_give, moved_d, moved_q, moved_conv, moved_out,
        *moved_full, moved_mix, moved_part, *moved_grad, *moved_swap,
    ):
        moved.wait_send()


def store(*refs):
    count = len(refs) // 2
    copies = [pltpu.make_async_copy(refs[i], refs[count + i], refs[-1].at[i]) for i in range(count)]
    for copy in copies:
        copy.start()
    for copy in copies:
        copy.wait()


def solution(mesh):
    ns, ny = mesh.shape["seq"], mesh.shape["ch"]
    nx, nz, _ = GRID[ns]

    def shards(q, k, v, f, w, g):
        rows, chans = q.shape
        width = g.shape[1]
        cut = width // (2 * nz)
        group = nx * 2
        run = nz * 4
        pieces = nz // 2
        table = tables(ns, rows, nx, nz)
        vm = pltpu.VMEM
        sizes = (nx, nz, ns, ny, rows, (ns * rows) ** -0.5)
        tok = lambda dtype: jax.ShapeDtypeStruct((rows, chans), dtype)
        results = pl.pallas_call(
            functools.partial(kernel, sizes),
            out_shape=(
                jax.ShapeDtypeStruct((rows, width), BF16), tok(BF16), tok(BF16), tok(BF16), tok(F32),
                jax.ShapeDtypeStruct((cut, chans), F32),
            ),
            in_specs=[pl.BlockSpec(memory_space=pl.ANY)] * 7,
            out_specs=(pl.BlockSpec(memory_space=pltpu.VMEM),) * 6,
            scratch_shapes=[
                vm(q.shape, BF16), vm(q.shape, BF16), vm(q.shape, BF16), vm(q.shape, BF16),
                vm(g.shape, BF16), vm(table.shape, F32),
                vm((2 * ns, 2 * ns), BF16), vm((6 * rows, 2 * rows), BF16), vm((6 * rows, 2 * rows), BF16),
                vm((ns, 6 * ns), BF16), vm((ns, 6 * ns), BF16), vm(w.shape, BF16),
                vm((ns, 16, rows), BF16), vm((ns, 16, rows), BF16),
                vm((nz, group * 8, rows), BF16), vm((nz, group * 8, rows), BF16),
                vm((chans, rows), F32), vm((ns // 2, 16, rows), BF16), vm((ns // 2, 16, rows), BF16),
                vm((ns // 4, 16, rows), BF16), vm((ns // 4, 16, rows), BF16),
                vm((ns, 16, rows), BF16), vm((ns, 16, rows), BF16),
                vm((ns * 16, rows), F32),
                vm((chans, 2 * rows), F32), vm((chans, 2 * rows), F32), vm((chans, 2 * rows), F32),
                vm((chans, 6 * rows), BF16),
                vm((pieces, ny, rows, width // pieces), BF16), vm((ny, 2, nz // 2, 2, cut, rows), BF16),
                vm((chans, rows), F32),
                vm((2, 2, nx, run, rows), BF16), vm((group, 2, run, rows), BF16),
                vm((group, 2, run, rows), BF16), vm((2, 2, nx, run, rows), BF16),
                vm((2, group, run, rows), BF16), vm((nx, 2, group, run, rows), BF16),
                vm((2, nx, 2, nz // 2, 2, cut, rows), BF16),
                vm((nz, 2, cut, 2 * run * nx), BF16), vm((2 * nz, cut, 2 * run * nx), BF16),
                vm((ny, rows, width), BF16), vm((ny, rows, width), BF16), vm((rows, width), F32),
                vm((chans, rows), F32),
                pltpu.SemaphoreType.DMA((7,)), pltpu.SemaphoreType.DMA((21,)), pltpu.SemaphoreType.DMA((21,)),
            ],
            compiler_params=pltpu.CompilerParams(
                collective_id=0, has_side_effects=True, vmem_limit_bytes=56 * 1024 * 1024
            ),
        )(q, k, v, f, w, g, table)
        *rest, gw = pl.pallas_call(
            store,
            out_shape=tuple(jax.ShapeDtypeStruct(r.shape, r.dtype) for r in results),
            in_specs=[pl.BlockSpec(memory_space=pltpu.VMEM)] * 6,
            out_specs=(pl.BlockSpec(memory_space=pl.ANY),) * 6,
            scratch_shapes=[pltpu.SemaphoreType.DMA((6,))],
        )(*results)
        return (*rest, gw.T)

    tokens = P("seq", "ch")
    return jax.shard_map(
        shards,
        mesh=mesh,
        in_specs=(tokens, tokens, tokens, tokens, P("ch", None), tokens),
        out_specs=(tokens, tokens, tokens, tokens, tokens, P("ch", "seq")),
        check_vma=False,
    )
```
